32 devices in a mesh: cls: 4 (over y, x), ptl: 8 (over z, core).
Axes of the slice: x: 2, y: 2, z: 4, core: 2. Of those that a mesh axis runs over, the one named last changes fastest.
Arguments:
- references: bfloat16 [4, 256, 4096], P('cls', 'ptl')
- particles: bfloat16 [16384, 4096], P(('cls', 'ptl'))
- class_ids: int32 [16384], P(('cls', 'ptl')), may hold values from 0 to 3, as said below
- orient_ids: int32 [16384], P(('cls', 'ptl')), may hold values from 0 to 255
- offsets: int32 [16384], P(('cls', 'ptl')), may hold values from -3 to 3
- weights: float32 [16384], P(('cls', 'ptl'))
Outputs:
- class_sums: float32 [4, 4096], P('cls', 'ptl')
The draws below stay inside these ranges and needn't reach their ends.
Inputs may be any that keep to these rules, and one draw needn't show every extreme that they name: `class_ids`: every class is the class of some particle; populations are uneven.
All inputs are finite; a program needn't handle non-finite values.
Results may differ from the reference program's by a relative error of at most 0.0028.
Values may be sent and summed in bfloat16 or wider, within the bound.
A program may use at most 64 MiB of HBM per device.

```python
import math
import jax
import jax.numpy as jnp
from jax import lax

NX = 64
NY = 64
ORI = 256
SHIFT = 3
CLASSES = 4
PARTICLES = 16384


def helper_refs(key):
    return jax.random.normal(jax.random.fold_in(key, 11), (CLASSES, ORI, NX * NY), jnp.float32)


def helper_classes(key):
    base = jax.random.fold_in(key, 12)
    first = jax.random.randint(jax.random.fold_in(base, 1), (PARTICLES,), 0, CLASSES)
    second = jax.random.randint(jax.random.fold_in(base, 2), (PARTICLES,), 0, CLASSES)
    order = jax.random.permutation(jax.random.fold_in(base, 3), CLASSES)
    return order[(first + 1) * second // CLASSES].astype(jnp.int32)


def helper_orients(key):
    return jax.random.randint(jax.random.fold_in(key, 13), (PARTICLES,), 0, ORI).astype(jnp.int32)


def draw_references(key, part):
    return helper_refs(key).astype(jnp.bfloat16)


def draw_class_ids(key, part):
    return helper_classes(key)


def draw_orient_ids(key, part):
    return helper_orients(key)


def draw_particles(key, part):
    voxels = NX * NY
    values = jax.random.normal(jax.random.fold_in(key, 14), (PARTICLES, voxels), jnp.float32)
    return values.astype(jnp.bfloat16)


def draw_weights(key, part):
    lows = jnp.log(jnp.float32(0.2))
    values = jnp.exp(jax.random.uniform(jax.random.fold_in(key, 18), (PARTICLES,), jnp.float32, lows, 0.0))
    return values


def plant(values, rng, smallest, largest):
    index_at = [jax.random.randint(jax.random.fold_in(rng, axis), (), 0, length) for axis, length in enumerate(values.shape)]
    widest = values.shape.index(max(values.shape))
    beside = index_at[:widest] + [(index_at[widest] + 1) % values.shape[widest]] + index_at[widest + 1:]
    return values.at[tuple(index_at)].set(smallest).at[tuple(beside)].set(largest)


def setup_inputs(seed: int = 0) -> dict:
    streams_of = jax.random.split(jax.random.key(seed), 7)
    references = draw_references(jax.random.fold_in(streams_of[6], 71), 0)
    particles = draw_particles(jax.random.fold_in(streams_of[6], 71), 0)
    class_ids = draw_class_ids(jax.random.fold_in(streams_of[6], 71), 0)
    orient_ids = draw_orient_ids(jax.random.fold_in(streams_of[6], 71), 0)
    offsets = plant(jax.random.randint(streams_of[4], (PARTICLES,), 0 - SHIFT, SHIFT + 1), jax.random.fold_in(streams_of[4], 1), 0 - SHIFT, SHIFT).astype(jnp.int32)
    weights = draw_weights(jax.random.fold_in(streams_of[6], 71), 0)
    return {"references": references, "particles": particles, "class_ids": class_ids, "orient_ids": orient_ids, "offsets": offsets, "weights": weights}


def reference(references, particles, class_ids, orient_ids, offsets, weights):
    classes, orients, voxels = references.shape
    rows = references.reshape(classes * orients, voxels)
    count = particles.shape[0]
    block = math.gcd(count, 1024)
    scale = 1.0 / math.sqrt(voxels)
    flat_ids = (class_ids * orients + orient_ids).astype(jnp.int32)

    def block_scores(args):
        part, picks = args
        scores = jnp.dot(part, rows.T, preferred_element_type=jnp.float32) * scale
        top = lax.optimization_barrier(jnp.max(scores, axis=1))
        total = lax.optimization_barrier(jnp.sum(jnp.exp(scores - top[:, None]), axis=1))
        chosen = jnp.take_along_axis(scores, picks[:, None], axis=1)[:, 0]
        return (top, total, chosen)
    top, total, chosen = lax.map(block_scores, (particles.reshape(count // block, block, voxels), flat_ids.reshape(count // block, block)))
    top = top.reshape(count)
    total = total.reshape(count)
    chosen = chosen.reshape(count)
    gain = (weights * (classes * orients) * jnp.exp(chosen - top) / total).astype(jnp.bfloat16)
    member = class_ids[None, :] == jnp.arange(classes, dtype=jnp.int32)[:, None]
    summed = jnp.zeros((classes, voxels), jnp.float32)
    for step in range(-SHIFT, SHIFT + 1):
        coef = jnp.where(member & (offsets[None, :] == step), gain[None, :], jnp.zeros((), gain.dtype))
        moved = jnp.dot(coef, particles, preferred_element_type=jnp.float32)
        moved = jnp.roll(moved.reshape(classes, voxels // NX, NX), step, axis=2).reshape(classes, voxels)
        summed = summed + moved
    return summed / jnp.sqrt(jnp.float32(count / classes))
```

```python
import functools
import math

import jax
import jax.numpy as jnp
from jax import lax
from jax.experimental import pallas as pl
from jax.experimental.pallas import tpu as pltpu
from jax.sharding import PartitionSpec as P

NX = 64
SHIFT = 3
MESH = pl.DeviceIdType.MESH

PLAN = (
    (
        (
            (0, 0, 1, 0), (0, 0, 0, 1), (0, 0, 0, 2), (0, 0, 0, 0), (0, 0, 1, 1),
            (0, 0, 1, 2), (0, 1, 0, -1), (2, 0, 0, -1), (1, 0, 1, -1), (2, 0, 0, 0),
            (1, 0, 1, 1), (0, 1, 0, 1), (0, 1, 1, -1), (2, 0, 1, -1), (1, 0, 0, -1),
            (0, 1, 1, 0),
        ),
        (
            (0, 1, 0, 0), (0, 1, 1, 1), (0, 2, 0, -1), (3, 0, 1, -1), (3, 0, 0, -1),
            (3, 0, 1, 2), (3, 0, 0, 2), (0, 2, 0, 0), (0, 2, 0, 1), (0, 2, 1, -1),
            (2, 1, 0, -1), (1, 1, 1, -1), (0, 2, 1, 0), (0, 2, 1, 1), (0, 3, 0, -1),
            (2, 1, 1, -1), (1, 1, 0, -1),
        ),
        (
            (2, 1, 0, 0), (1, 1, 1, 1), (0, 3, 1, -1), (2, 2, 0, -1), (1, 2, 0, -1),
            (0, 3, 0, 0), (0, 3, 0, 1), (3, 2, 0, -1), (2, 2, 1, -1), (1, 2, 1, -1),
            (0, 3, 1, 0), (0, 3, 1, 1), (3, 3, 1, -1), (3, 1, 1, -1), (3, 1, 0, -1),
        ),
        (
            (3, 2, 1, -1), (2, 3, 0, -1), (1, 3, 0, -1), (3, 3, 0, -1), (2, 3, 1, -1),
            (1, 3, 1, -1),
        ),
    ),
    (
        (
            (0, 1, 1, 0), (0, 1, 0, 1), (0, 1, 0, 2), (0, 1, 0, 3), (0, 1, 0, 0),
            (0, 1, 1, 1), (0, 1, 1, 2), (0, 1, 1, 3), (0, 0, 0, -1), (0, 2, 0, -1),
            (2, 1, 0, -1), (1, 1, 1, -1), (0, 0, 0, 0), (0, 2, 0, 1), (0, 0, 0, 2),
            (0, 2, 0, 3), (0, 0, 0, 1), (0, 0, 1, -1), (0, 2, 1, -1), (2, 1, 1, -1),
            (1, 1, 0, -1), (0, 2, 1, 0), (0, 0, 1, 2), (0, 2, 1, 3),
        ),
        (
            (1, 1, 1, 1), (0, 3, 0, -1), (2, 2, 0, -1), (1, 0, 0, -1), (2, 2, 0, 0),
            (0, 3, 0, 3), (0, 2, 0, 0), (0, 3, 1, -1), (2, 0, 0, -1), (1, 2, 1, -1),
            (1, 2, 1, 1), (0, 3, 1, 3), (3, 0, 1, -1), (3, 0, 1, 2), (2, 1, 0, 0),
            (0, 0, 1, 1), (3, 1, 1, -1), (3, 2, 0, -1), (3, 2, 0, 3), (3, 0, 0, -1),
            (3, 0, 0, 2), (3, 3, 1, -1), (0, 0, 1, 0), (0, 2, 1, 1), (3, 3, 1, 3),
            (3, 2, 1, -1), (1, 2, 0, -1), (3, 3, 0, -1),
        ),
        (
            (0, 3, 0, 0), (0, 3, 0, 1), (3, 2, 1, 3), (2, 0, 1, -1), (3, 1, 0, -1),
            (0, 3, 1, 0), (0, 3, 1, 1), (3, 3, 0, 3), (2, 2, 1, -1), (1, 0, 1, -1),
        ),
        (
            (2, 3, 0, -1), (1, 3, 0, -1), (2, 3, 1, -1), (1, 3, 1, -1),
        ),
    ),
)

GROUPS = (
    (
        ((0, 0), (0, 1), (2, 0), (1, 0)),
        ((3, 0), (0, 2), (2, 1), (1, 1)),
        ((0, 3), (2, 2), (1, 2), (3, 1)),
        ((3, 2), (2, 3), (1, 3), (3, 3)),
    ),
    (
        ((0, 1), (0, 0), (0, 2), (2, 1)),
        ((1, 1), (0, 3), (3, 0), (1, 2)),
        ((3, 2), (3, 3), (2, 0), (3, 1)),
        ((2, 2), (1, 0), (2, 3), (1, 3)),
    ),
)
DEPTH = 1024
ROWS = 8


def kernel(
    orients, population,
    refs, parts, cid, oid, off, wts, out,
    rows, pv, top_s, tot_s, cho_s, part, recv1, send2, recv2,
    local_sem, ici_sem, sib_sem, send_sem, r1_sem, r2_sem, s1_sem, s2_sem,
):
    n_cls, n_ptl = part.shape[0], part.shape[1]
    voxels = refs.shape[2]
    half = pv.shape[1]
    cls, ptl = lax.axis_index("cls"), lax.axis_index("ptl")
    core, z = ptl % 2, ptl // 2
    far = z // 2
    sign = 1 - 2 * far
    place = z + far * (3 - 2 * z)
    along_x = cls + 1 - 2 * (cls % 2)
    along_y = cls + 2 - 4 * (cls // 2)
    column = (cls, along_x, along_y, 3 - cls)
    sibling = (cls, ptl + 1 - 2 * core)
    ways = (
        (along_x, ptl),
        (along_y, ptl),
        (cls, ptl + 2 * sign),
        (cls, ptl - 2 * sign),
    )

    def pair(q, zz):
        return column[q] * 4 + zz + far * (3 - 2 * zz)

    barrier = pltpu.get_barrier_semaphore()
    for q in (1, 2, 3):
        pl.semaphore_signal(barrier, inc=1, device_id=(column[q], ptl), device_id_type=MESH)
    for o in range(1, n_ptl):
        pl.semaphore_signal(
            barrier, inc=1, device_id=(cls, lax.rem(ptl + o, n_ptl)), device_id_type=MESH
        )
    loads = [
        pltpu.make_async_copy(parts.at[pl.ds(i * half, half)], pv.at[i], local_sem.at[i])
        for i in range(2)
    ]
    own = cls * 4 + z
    for h in range(2):
        loads.append(
            pltpu.make_async_copy(
                refs.at[0, pl.ds(16 * h, 16)], rows.at[own, core, h], local_sem.at[2 + h]
            )
        )
    for load in loads:
        load.start()
    pl.semaphore_wait(barrier, 3 + n_ptl - 1)

    def send(src, p, h, way):
        target, recv, idx = (
            (sibling, sib_sem, 4) if way == 4 else (ways[way], ici_sem, way)
        )
        pltpu.make_async_remote_copy(
            src_ref=src,
            dst_ref=rows.at[p, core, h],
            send_sem=send_sem.at[idx],
            recv_sem=recv.at[p, h],
            device_id=target,
            device_id_type=MESH,
        ).start()

    def run(section):
        for q, zz, h, way in section:
            p = pair(q, zz)
            block = rows.at[p, core, h]
            if way < 0:
                pltpu.make_async_copy(block, block, ici_sem.at[p, h]).wait()
                send(block, p, h, 4)
            elif q == 0 and p_own(zz):
                send(refs.at[0, pl.ds(16 * h, 16)], p, h, way)
            else:
                send(block, p, h, way)

    top_s[...] = jnp.full(top_s.shape, -jnp.inf, jnp.float32)
    tot_s[...] = jnp.zeros(tot_s.shape, jnp.float32)
    cho_s[...] = jnp.zeros(cho_s.shape, jnp.float32)

    for s in range(4):
        for zc in range(2):
            def p_own(zz, zc=zc):
                return zz == zc

            def branch(s=s, zc=zc):
                if s == 0:
                    first = [e for e in PLAN[zc][0] if e[0] == 0 and e[1] == zc]
                    rest = [e for e in PLAN[zc][0] if not (e[0] == 0 and e[1] == zc)]
                    run(first)
                    for h in range(2):
                        send(refs.at[0, pl.ds(16 * h, 16)], own, h, 4)
                    run(rest)
                else:
                    run(PLAN[zc][s])

            pl.when(place == zc)(branch)
        if s == 0:
            for load in loads:
                load.wait()
        group = []
        for a, b in zip(GROUPS[0][s], GROUPS[1][s]):
            group.append(jnp.where(place == 0, pair(*a), pair(*b)))
        for p in group:
            for h in range(2):
                block = rows.at[p, 1 - core, h]
                pltpu.make_async_copy(block, block, sib_sem.at[p, h]).wait()

        def scores(n, _, group=group):
            acc = jnp.zeros((4 * 64, half), jnp.float32)
            for k in range(0, voxels, DEPTH):
                lhs = jnp.concatenate(
                    [rows[p, :, :, :, k : k + DEPTH].reshape(64, DEPTH) for p in group], axis=0
                )
                acc += lax.dot_general(
                    lhs,
                    pv[n, :, k : k + DEPTH],
                    (((1,), (1,)), ((), ())),
                    preferred_element_type=jnp.float32,
                )
            sc = acc * (1.0 / math.sqrt(voxels))
            cols = pl.ds(pl.multiple_of(n * half, half), half)
            old = top_s[:, cols]
            new = jnp.maximum(old, jnp.max(sc, axis=0, keepdims=True))
            top_s[:, cols] = new
            tot_s[:, cols] = tot_s[:, cols] * jnp.exp(old - new) + jnp.sum(
                jnp.exp(sc - new), axis=0, keepdims=True
            )
            wanted = cid[:, cols] * orients + oid[:, cols]
            inner = lax.broadcasted_iota(jnp.int32, (64, half), 0)
            picked = jnp.zeros((1, half), jnp.float32)
            for i, p in enumerate(group):
                mine = inner == wanted - p * 64
                picked += jnp.sum(
                    jnp.where(mine, sc[64 * i : 64 * i + 64], 0.0), axis=0, keepdims=True
                )
            cho_s[:, cols] += picked
            return _

        lax.fori_loop(0, 2, scores, 0)

    gain = wts[...] * (n_cls * orients) * jnp.exp(cho_s[...] - top_s[...]) / tot_s[...]
    gain = gain.astype(jnp.bfloat16).astype(jnp.float32)
    code = (off[...] + SHIFT) * ROWS + cid[...]
    steps = 2 * SHIFT + 1
    which = lax.broadcasted_iota(jnp.int32, (steps * ROWS, 2 * half), 0)
    coef = jnp.where(which == code, gain, 0.0).astype(jnp.bfloat16)
    width = voxels // n_ptl
    lane = lax.broadcasted_iota(jnp.int32, (ROWS, 128), 1) % NX
    for j in range(n_ptl):
        pixels = pv[:, :, j * width : (j + 1) * width].reshape(2 * half, width)
        moved = jnp.dot(coef, pixels, preferred_element_type=jnp.float32)
        for v in range(width // 128):
            total = jnp.zeros((ROWS, 128), jnp.float32)
            for i, step in enumerate(range(-SHIFT, SHIFT + 1)):
                a = moved[i * ROWS : (i + 1) * ROWS, v * 128 : (v + 1) * 128]
                if step == 0:
                    total += a
                    continue
                inside = pltpu.roll(a, step % 128, 1)
                across = pltpu.roll(a, (step + NX) % 128, 1)
                keep = lane >= step if step > 0 else lane < NX + step
                total += jnp.where(keep, inside, across)
            for c in range(n_cls):
                part[c, j : j + 1, v * 128 : (v + 1) * 128] = total[c : c + 1]

    copies = []
    for q in (1, 2, 3):
        copies.append(
            pltpu.make_async_remote_copy(
                src_ref=part.at[column[q]],
                dst_ref=recv1.at[q - 1],
                send_sem=s1_sem.at[q - 1],
                recv_sem=r1_sem.at[q - 1],
                device_id=(column[q], ptl),
                device_id_type=MESH,
            )
        )
        copies[-1].start()
    for copy in copies:
        copy.wait_recv()
    mine = part[cls] + recv1[0] + recv1[1] + recv1[2]
    for j in range(n_ptl):
        send2[j] = mine[j : j + 1]
    for o in range(1, n_ptl):
        to = lax.rem(ptl + o, n_ptl)
        copies.append(
            pltpu.make_async_remote_copy(
                src_ref=send2.at[to],
                dst_ref=recv2.at[o - 1],
                send_sem=s2_sem.at[o - 1],
                recv_sem=r2_sem.at[o - 1],
                device_id=(cls, to),
                device_id_type=MESH,
            )
        )
        copies[-1].start()
    total = send2[ptl]
    for o in range(1, n_ptl):
        copies[2 + o].wait_recv()
        total += recv2[o - 1]
    out[...] = total / jnp.sqrt(jnp.float32(population))
    for copy in copies:
        copy.wait_send()

    def sent(count, idx):
        gone = rows.at[pl.ds(0, count), 0]
        pltpu.make_async_copy(gone, gone, send_sem.at[idx]).wait()

    sent(5, 0)
    sent(5, 1)
    sent(16, 4)

    @pl.when(place == 0)
    def _():
        sent(2, 2)

    @pl.when(place == 1)
    def _():
        sent(3, 2)
        sent(5, 3)


def fused(references, particles, class_ids, orient_ids, offsets, weights):
    n_cls = lax.axis_size("cls")
    n_ptl = lax.axis_size("ptl")
    _, local_ori, voxels = references.shape
    count = particles.shape[0]
    orients = local_ori * n_ptl
    population = count * n_ptl
    line = [x.reshape(1, count) for x in (class_ids, orient_ids, offsets, weights)]
    f32 = jnp.float32
    vmem = pl.BlockSpec(memory_space=pltpu.VMEM)
    hbm = pl.BlockSpec(memory_space=pl.ANY)
    return pl.pallas_call(
        functools.partial(kernel, orients, population),
        out_shape=jax.ShapeDtypeStruct((1, voxels // n_ptl), f32),
        in_specs=[hbm, hbm, vmem, vmem, vmem, vmem],
        out_specs=vmem,
        scratch_shapes=[
            pltpu.VMEM((n_cls * n_ptl // 2, 2, 2, local_ori // 2, voxels), references.dtype),
            pltpu.VMEM((2, count // 2, voxels), particles.dtype),
            pltpu.VMEM((1, count), f32),
            pltpu.VMEM((1, count), f32),
            pltpu.VMEM((1, count), f32),
            pltpu.VMEM((n_cls, n_ptl, voxels // n_ptl), f32),
            pltpu.VMEM((n_cls - 1, n_ptl, voxels // n_ptl), f32),
            pltpu.VMEM((n_ptl, 1, voxels // n_ptl), f32),
            pltpu.VMEM((n_ptl - 1, 1, voxels // n_ptl), f32),
            pltpu.SemaphoreType.DMA((4,)),
            pltpu.SemaphoreType.DMA((n_cls * n_ptl // 2, 2)),
            pltpu.SemaphoreType.DMA((n_cls * n_ptl // 2, 2)),
            pltpu.SemaphoreType.DMA((5,)),
            pltpu.SemaphoreType.DMA((n_cls - 1,)),
            pltpu.SemaphoreType.DMA((n_ptl - 1,)),
            pltpu.SemaphoreType.DMA((n_cls - 1,)),
            pltpu.SemaphoreType.DMA((n_ptl - 1,)),
        ],
        compiler_params=pltpu.CompilerParams(
            collective_id=0, has_side_effects=True, vmem_limit_bytes=40 * 1024 * 1024
        ),
        cost_estimate=pl.CostEstimate(
            flops=2 * count * voxels * n_cls * orients,
            bytes_accessed=2 * voxels * (count + n_cls * orients),
            transcendentals=count * n_cls * orients,
        ),
    )(references, particles, *line)


def body(references, particles, class_ids, orient_ids, offsets, weights):
    n_cls = lax.axis_size("cls")
    n_ptl = lax.axis_size("ptl")
    per_owner, local_ori, voxels = references.shape
    orients = local_ori * n_ptl
    classes = per_owner * n_cls
    count = particles.shape[0]
    scale = 1.0 / math.sqrt(voxels)
    class_block = lax.all_gather(references, "ptl", axis=1, tiled=True)
    piece = lax.all_gather(class_block, "cls", axis=0, tiled=True)
    rows = piece.reshape(piece.shape[0] * orients, voxels)
    place = jnp.arange(rows.shape[0], dtype=jnp.int32)
    top = jnp.full((count,), -1e30, jnp.float32)
    scores = (
        lax.dot_general(
            particles, rows, (((1,), (1,)), ((), ())), preferred_element_type=jnp.float32
        )
        * scale
    )
    newtop = jnp.maximum(top, jnp.max(scores, axis=1))
    total = jnp.sum(jnp.exp(scores - newtop[:, None]), axis=1)
    picked = (class_ids[:, None] == (place // orients)[None, :]) & (
        orient_ids[:, None] == (place % orients)[None, :]
    )
    chosen = jnp.sum(jnp.where(picked, scores, 0.0), axis=1)
    top, total, chosen = (newtop, total, chosen)
    gain = (weights * (classes * orients) * jnp.exp(chosen - top) / total).astype(jnp.bfloat16)
    member = class_ids[None, :] == jnp.arange(classes, dtype=jnp.int32)[:, None]
    partial_sums = jnp.zeros((classes, voxels), jnp.float32)
    for step in range(-SHIFT, SHIFT + 1):
        coef = jnp.where(
            member & (offsets[None, :] == step), gain[None, :], jnp.zeros((), jnp.bfloat16)
        )
        moved = jnp.dot(coef, particles, preferred_element_type=jnp.float32)
        moved = jnp.roll(moved.reshape(classes, voxels // NX, NX), step, axis=2).reshape(
            classes, voxels
        )
        partial_sums = partial_sums + moved
    owned = lax.psum_scatter(partial_sums, "cls", scatter_dimension=0, tiled=True)
    owned = lax.psum_scatter(owned, "ptl", scatter_dimension=1, tiled=True)
    population = count * n_cls * n_ptl / classes
    return owned / jnp.sqrt(jnp.float32(population))


def solution(mesh):
    placed = (
        P("cls", "ptl", None),
        P(("cls", "ptl"), None),
        P(("cls", "ptl")),
        P(("cls", "ptl")),
        P(("cls", "ptl")),
        P(("cls", "ptl")),
    )
    planned = mesh.shape["cls"] == 4 and mesh.shape["ptl"] == 8
    return jax.shard_map(
        fused if planned else body,
        mesh=mesh,
        in_specs=placed,
        out_specs=P("cls", "ptl"),
        check_vma=False,
    )
```

```python
import functools
import math

import jax
import jax.numpy as jnp
from jax import lax
from jax.experimental import pallas as pl
from jax.experimental.pallas import tpu as pltpu
from jax.sharding import PartitionSpec as P

NX = 64
SHIFT = 3
MESH = pl.DeviceIdType.MESH

PLAN = (
    (
        (
            (0, 0, 1, 0), (0, 0, 0, 1), (0, 0, 0, 2), (0, 0, 0, 0), (0, 0, 1, 1), (0, 0, 1, 2),
        ),
        (
            (0, 1, 0, -1), (2, 0, 0, -1), (1, 0, 1, -1), (2, 0, 0, 0), (1, 0, 1, 1),
        ),
        (
            (0, 1, 0, 1), (0, 1, 1, -1), (2, 0, 1, -1), (1, 0, 0, -1), (0, 1, 1, 0),
        ),
        (
            (0, 1, 0, 0), (0, 1, 1, 1), (0, 2, 0, -1), (3, 0, 1, -1), (3, 0, 0, -1), (3, 0, 1, 2),
            (3, 0, 0, 2),
        ),
        (
            (0, 2, 0, 0), (0, 2, 0, 1), (0, 2, 1, -1), (2, 1, 0, -1), (1, 1, 1, -1),
        ),
        (
            (0, 2, 1, 0), (0, 2, 1, 1), (0, 3, 0, -1), (2, 1, 1, -1), (1, 1, 0, -1),
        ),
        (
            (2, 1, 0, 0), (1, 1, 1, 1), (0, 3, 1, -1), (2, 2, 0, -1), (1, 2, 0, -1),
        ),
        (
            (0, 3, 0, 0), (0, 3, 0, 1), (3, 2, 0, -1), (2, 2, 1, -1), (1, 2, 1, -1),
        ),
        (
            (0, 3, 1, 0), (0, 3, 1, 1), (3, 3, 1, -1), (3, 1, 1, -1), (3, 1, 0, -1),
        ),
        (
            (3, 2, 1, -1), (2, 3, 0, -1), (1, 3, 0, -1),
        ),
        (
            (3, 3, 0, -1), (2, 3, 1, -1), (1, 3, 1, -1),
        ),
    ),
    (
        (
            (0, 1, 1, 0), (0, 1, 0, 1), (0, 1, 0, 2), (0, 1, 0, 3), (0, 1, 0, 0), (0, 1, 1, 1),
            (0, 1, 1, 2), (0, 1, 1, 3),
        ),
        (
            (0, 0, 0, -1), (0, 2, 0, -1), (2, 1, 0, -1), (1, 1, 1, -1), (0, 0, 0, 0), (0, 2, 0, 1),
            (0, 0, 0, 2), (0, 2, 0, 3),
        ),
        (
            (0, 0, 0, 1), (0, 0, 1, -1), (0, 2, 1, -1), (2, 1, 1, -1), (1, 1, 0, -1), (0, 2, 1, 0),
            (0, 0, 1, 2), (0, 2, 1, 3),
        ),
        (
            (1, 1, 1, 1), (0, 3, 0, -1), (2, 2, 0, -1), (1, 0, 0, -1), (2, 2, 0, 0), (0, 3, 0, 3),
        ),
        (
            (0, 2, 0, 0), (0, 3, 1, -1), (2, 0, 0, -1), (1, 2, 1, -1), (1, 2, 1, 1), (0, 3, 1, 3),
            (3, 0, 1, -1), (3, 0, 1, 2),
        ),
        (
            (2, 1, 0, 0), (0, 0, 1, 1), (3, 1, 1, -1), (3, 2, 0, -1), (3, 2, 0, 3), (3, 0, 0, -1),
            (3, 0, 0, 2), (3, 3, 1, -1),
        ),
        (
            (0, 0, 1, 0), (0, 2, 1, 1), (3, 3, 1, 3), (3, 2, 1, -1), (1, 2, 0, -1), (3, 3, 0, -1),
        ),
        (
            (0, 3, 0, 0), (0, 3, 0, 1), (3, 2, 1, 3), (2, 0, 1, -1), (3, 1, 0, -1),
        ),
        (
            (0, 3, 1, 0), (0, 3, 1, 1), (3, 3, 0, 3), (2, 2, 1, -1), (1, 0, 1, -1),
        ),
        (
            (2, 3, 0, -1), (1, 3, 0, -1),
        ),
        (
            (2, 3, 1, -1), (1, 3, 1, -1),
        ),
    ),
)

GROUPS = (
    (
        ((0, 0), (0, 1), (2, 0), (1, 0)),
        ((3, 0), (0, 2), (2, 1), (1, 1)),
        ((0, 3), (2, 2), (1, 2), (3, 1)),
        ((3, 2), (2, 3), (1, 3), (3, 3)),
    ),
    (
        ((0, 1), (0, 0), (0, 2), (2, 1)),
        ((1, 1), (0, 3), (3, 0), (1, 2)),
        ((3, 2), (3, 3), (2, 0), (3, 1)),
        ((2, 2), (1, 0), (2, 3), (1, 3)),
    ),
)
UNITS = ((), (), ((0, 0),), ((0, 1),), (), (), ((1, 0),), ((1, 1),), ((2, 0),), ((2, 1),), ((3, 0), (3, 1)))
DEPTH = 1024
ROWS = 8


def kernel(
    orients, population,
    refs, parts, cid_in, oid_in, off_in, wts_in, out,
    rows, pv, cid, oid, off, wts, top_s, tot_s, cho_s, part, recv1, send2, recv2,
    local_sem, ici_sem, sib_sem, send_sem, r1_sem, r2_sem, s1_sem, s2_sem,
):
    n_cls, n_ptl = part.shape[0], part.shape[1]
    voxels = refs.shape[2]
    half = pv.shape[1]
    cls, ptl = lax.axis_index("cls"), lax.axis_index("ptl")
    core, z = ptl % 2, ptl // 2
    far = z // 2
    sign = 1 - 2 * far
    place = z + far * (3 - 2 * z)
    along_x = cls + 1 - 2 * (cls % 2)
    along_y = cls + 2 - 4 * (cls // 2)
    column = (cls, along_x, along_y, 3 - cls)
    sibling = (cls, ptl + 1 - 2 * core)
    ways = (
        (along_x, ptl),
        (along_y, ptl),
        (cls, ptl + 2 * sign),
        (cls, ptl - 2 * sign),
    )

    def pair(q, zz):
        return column[q] * 4 + zz + far * (3 - 2 * zz)

    barrier = pltpu.get_barrier_semaphore()
    for q in (1, 2, 3):
        pl.semaphore_signal(barrier, inc=1, device_id=(column[q], ptl), device_id_type=MESH)
    for o in range(1, n_ptl):
        pl.semaphore_signal(
            barrier, inc=1, device_id=(cls, lax.rem(ptl + o, n_ptl)), device_id_type=MESH
        )
    loads = [
        pltpu.make_async_copy(parts.at[pl.ds(i * half, half)], pv.at[i], local_sem.at[i])
        for i in range(2)
    ]
    own = cls * 4 + z
    for h in range(2):
        loads.append(
            pltpu.make_async_copy(
                refs.at[0, pl.ds(16 * h, 16)], rows.at[own, core, h], local_sem.at[2 + h]
            )
        )
    for i, (a, b) in enumerate(((cid_in, cid), (oid_in, oid), (off_in, off), (wts_in, wts))):
        loads.append(pltpu.make_async_copy(a, b, local_sem.at[4 + i]))
    for load in loads:
        load.start()
    pl.semaphore_wait(barrier, 3 + n_ptl - 1)

    def send(src, p, h, way):
        target, recv, idx = (
            (sibling, sib_sem, 4) if way == 4 else (ways[way], ici_sem, way)
        )
        pltpu.make_async_remote_copy(
            src_ref=src,
            dst_ref=rows.at[p, core, h],
            send_sem=send_sem.at[idx],
            recv_sem=recv.at[p, h],
            device_id=target,
            device_id_type=MESH,
        ).start()

    def run(section, zc):
        for q, zz, h, way in section:
            p = pair(q, zz)
            block = rows.at[p, core, h]
            if way < 0:
                pltpu.make_async_copy(block, block, ici_sem.at[p, h]).wait()
                send(block, p, h, 4)
            elif q == 0 and zz == zc:
                send(refs.at[0, pl.ds(16 * h, 16)], p, h, way)
            else:
                send(block, p, h, way)

    top_s[...] = jnp.full(top_s.shape, -jnp.inf, jnp.float32)
    tot_s[...] = jnp.zeros(tot_s.shape, jnp.float32)
    cho_s[...] = jnp.zeros(cho_s.shape, jnp.float32)

    def scores(n, group):
        acc = jnp.zeros((len(group) * 64, half), jnp.float32)
        for k in range(0, voxels, DEPTH):
            lhs = jnp.concatenate(
                [rows[p, :, :, :, k : k + DEPTH].reshape(64, DEPTH) for p in group], axis=0
            )
            acc += lax.dot_general(
                lhs,
                pv[n, :, k : k + DEPTH],
                (((1,), (1,)), ((), ())),
                preferred_element_type=jnp.float32,
            )
        sc = acc * (1.0 / math.sqrt(voxels))
        cols = pl.ds(n * half, half)
        old = top_s[:, cols]
        new = jnp.maximum(old, jnp.max(sc, axis=0, keepdims=True))
        top_s[:, cols] = new
        tot_s[:, cols] = tot_s[:, cols] * jnp.exp(old - new) + jnp.sum(
            jnp.exp(sc - new), axis=0, keepdims=True
        )
        wanted = cid[:, cols] * orients + oid[:, cols]
        inner = lax.broadcasted_iota(jnp.int32, (64, half), 0)
        picked = jnp.zeros((1, half), jnp.float32)
        for i, p in enumerate(group):
            mine = inner == wanted - p * 64
            picked += jnp.sum(
                jnp.where(mine, sc[64 * i : 64 * i + 64], 0.0), axis=0, keepdims=True
            )
        cho_s[:, cols] += picked

    groups = [
        [jnp.where(place == 0, pair(*a), pair(*b)) for a, b in zip(first, second)]
        for first, second in zip(*GROUPS)
    ]
    for s, units in enumerate(UNITS):
        for zc in range(2):

            def branch(s=s, zc=zc):
                run(PLAN[zc][s], zc)
                if s == 0:
                    for h in range(2):
                        send(refs.at[0, pl.ds(16 * h, 16)], own, h, 4)

            pl.when(place == zc)(branch)
        if s == 0:
            for load in loads:
                load.wait()
        for g, n in units:
            if n == 0:
                for p in groups[g]:
                    for h in range(2):
                        block = rows.at[p, 1 - core, h]
                        pltpu.make_async_copy(block, block, sib_sem.at[p, h]).wait()
            scores(n, groups[g])

    gain = wts[...] * (n_cls * orients) * jnp.exp(cho_s[...] - top_s[...]) / tot_s[...]
    gain = gain.astype(jnp.bfloat16).astype(jnp.float32)
    code = (off[...] + SHIFT) * ROWS + cid[...]
    steps = 2 * SHIFT + 1
    which = lax.broadcasted_iota(jnp.int32, (steps * ROWS, 2 * half), 0)
    coef = jnp.where(which == code, gain, 0.0).astype(jnp.bfloat16)
    width = voxels // n_ptl
    lane = lax.broadcasted_iota(jnp.int32, (ROWS, 128), 1) % NX
    for j in range(n_ptl):
        pixels = pv[:, :, j * width : (j + 1) * width].reshape(2 * half, width)
        moved = jnp.dot(coef, pixels, preferred_element_type=jnp.float32)
        for v in range(width // 128):
            total = jnp.zeros((ROWS, 128), jnp.float32)
            for i, step in enumerate(range(-SHIFT, SHIFT + 1)):
                a = moved[i * ROWS : (i + 1) * ROWS, v * 128 : (v + 1) * 128]
                if step == 0:
                    total += a
                    continue
                inside = pltpu.roll(a, step % 128, 1)
                across = pltpu.roll(a, (step + NX) % 128, 1)
                keep = lane >= step if step > 0 else lane < NX + step
                total += jnp.where(keep, inside, across)
            for c in range(n_cls):
                part[c, j : j + 1, v * 128 : (v + 1) * 128] = total[c : c + 1]

    copies = []
    for q in (1, 2, 3):
        copies.append(
            pltpu.make_async_remote_copy(
                src_ref=part.at[column[q]],
                dst_ref=recv1.at[q - 1],
                send_sem=s1_sem.at[q - 1],
                recv_sem=r1_sem.at[q - 1],
                device_id=(column[q], ptl),
                device_id_type=MESH,
            )
        )
        copies[-1].start()
    for copy in copies:
        copy.wait_recv()
    mine = part[cls] + recv1[0] + recv1[1] + recv1[2]
    for j in range(n_ptl):
        send2[j] = mine[j : j + 1]
    for o in range(1, n_ptl):
        to = lax.rem(ptl + o, n_ptl)
        copies.append(
            pltpu.make_async_remote_copy(
                src_ref=send2.at[to],
                dst_ref=recv2.at[o - 1],
                send_sem=s2_sem.at[o - 1],
                recv_sem=r2_sem.at[o - 1],
                device_id=(cls, to),
                device_id_type=MESH,
            )
        )
        copies[-1].start()
    total = send2[ptl]
    for o in range(1, n_ptl):
        copies[2 + o].wait_recv()
        total += recv2[o - 1]
    out[...] = total / jnp.sqrt(jnp.float32(population))
    for copy in copies:
        copy.wait_send()

    def sent(count, idx):
        gone = rows.at[pl.ds(0, count), 0]
        pltpu.make_async_copy(gone, gone, send_sem.at[idx]).wait()

    sent(5, 0)
    sent(5, 1)
    sent(16, 4)

    @pl.when(place == 0)
    def _():
        sent(2, 2)

    @pl.when(place == 1)
    def _():
        sent(3, 2)
        sent(5, 3)


def fused(references, particles, class_ids, orient_ids, offsets, weights):
    n_cls = lax.axis_size("cls")
    n_ptl = lax.axis_size("ptl")
    _, local_ori, voxels = references.shape
    count = particles.shape[0]
    orients = local_ori * n_ptl
    population = count * n_ptl
    line = [x.reshape(1, count) for x in (class_ids, orient_ids, offsets, weights)]
    f32 = jnp.float32
    vmem = pl.BlockSpec(memory_space=pltpu.VMEM)
    hbm = pl.BlockSpec(memory_space=pl.ANY)
    return pl.pallas_call(
        functools.partial(kernel, orients, population),
        out_shape=jax.ShapeDtypeStruct((1, voxels // n_ptl), f32),
        in_specs=[hbm] * 6,
        out_specs=vmem,
        scratch_shapes=[
            pltpu.VMEM((n_cls * n_ptl // 2, 2, 2, local_ori // 2, voxels), references.dtype),
            pltpu.VMEM((2, count // 2, voxels), particles.dtype),
            *[pltpu.VMEM((1, count), x.dtype) for x in line],
            pltpu.VMEM((1, count), f32),
            pltpu.VMEM((1, count), f32),
            pltpu.VMEM((1, count), f32),
            pltpu.VMEM((n_cls, n_ptl, voxels // n_ptl), f32),
            pltpu.VMEM((n_cls - 1, n_ptl, voxels // n_ptl), f32),
            pltpu.VMEM((n_ptl, 1, voxels // n_ptl), f32),
            pltpu.VMEM((n_ptl - 1, 1, voxels // n_ptl), f32),
            pltpu.SemaphoreType.DMA((8,)),
            pltpu.SemaphoreType.DMA((n_cls * n_ptl // 2, 2)),
            pltpu.SemaphoreType.DMA((n_cls * n_ptl // 2, 2)),
            pltpu.SemaphoreType.DMA((5,)),
            pltpu.SemaphoreType.DMA((n_cls - 1,)),
            pltpu.SemaphoreType.DMA((n_ptl - 1,)),
            pltpu.SemaphoreType.DMA((n_cls - 1,)),
            pltpu.SemaphoreType.DMA((n_ptl - 1,)),
        ],
        compiler_params=pltpu.CompilerParams(
            collective_id=0, has_side_effects=True, vmem_limit_bytes=60 * 1024 * 1024
        ),
        cost_estimate=pl.CostEstimate(
            flops=2 * count * voxels * n_cls * orients,
            bytes_accessed=2 * voxels * (count + n_cls * orients),
            transcendentals=count * n_cls * orients,
        ),
    )(references, particles, *line)


def body(references, particles, class_ids, orient_ids, offsets, weights):
    n_cls = lax.axis_size("cls")
    n_ptl = lax.axis_size("ptl")
    per_owner, local_ori, voxels = references.shape
    orients = local_ori * n_ptl
    classes = per_owner * n_cls
    count = particles.shape[0]
    scale = 1.0 / math.sqrt(voxels)
    class_block = lax.all_gather(references, "ptl", axis=1, tiled=True)
    piece = lax.all_gather(class_block, "cls", axis=0, tiled=True)
    rows = piece.reshape(piece.shape[0] * orients, voxels)
    place = jnp.arange(rows.shape[0], dtype=jnp.int32)
    top = jnp.full((count,), -1e30, jnp.float32)
    scores = (
        lax.dot_general(
            particles, rows, (((1,), (1,)), ((), ())), preferred_element_type=jnp.float32
        )
        * scale
    )
    newtop = jnp.maximum(top, jnp.max(scores, axis=1))
    total = jnp.sum(jnp.exp(scores - newtop[:, None]), axis=1)
    picked = (class_ids[:, None] == (place // orients)[None, :]) & (
        orient_ids[:, None] == (place % orients)[None, :]
    )
    chosen = jnp.sum(jnp.where(picked, scores, 0.0), axis=1)
    top, total, chosen = (newtop, total, chosen)
    gain = (weights * (classes * orients) * jnp.exp(chosen - top) / total).astype(jnp.bfloat16)
    member = class_ids[None, :] == jnp.arange(classes, dtype=jnp.int32)[:, None]
    partial_sums = jnp.zeros((classes, voxels), jnp.float32)
    for step in range(-SHIFT, SHIFT + 1):
        coef = jnp.where(
            member & (offsets[None, :] == step), gain[None, :], jnp.zeros((), jnp.bfloat16)
        )
        moved = jnp.dot(coef, particles, preferred_element_type=jnp.float32)
        moved = jnp.roll(moved.reshape(classes, voxels // NX, NX), step, axis=2).reshape(
            classes, voxels
        )
        partial_sums = partial_sums + moved
    owned = lax.psum_scatter(partial_sums, "cls", scatter_dimension=0, tiled=True)
    owned = lax.psum_scatter(owned, "ptl", scatter_dimension=1, tiled=True)
    population = count * n_cls * n_ptl / classes
    return owned / jnp.sqrt(jnp.float32(population))


def solution(mesh):
    placed = (
        P("cls", "ptl", None),
        P(("cls", "ptl"), None),
        P(("cls", "ptl")),
        P(("cls", "ptl")),
        P(("cls", "ptl")),
        P(("cls", "ptl")),
    )
    planned = mesh.shape["cls"] == 4 and mesh.shape["ptl"] == 8
    return jax.shard_map(
        fused if planned else body,
        mesh=mesh,
        in_specs=placed,
        out_specs=P("cls", "ptl"),
        check_vma=False,
    )
```

```python
import functools
import math

import jax
import jax.numpy as jnp
from jax import lax
from jax.experimental import pallas as pl
from jax.experimental.pallas import tpu as pltpu
from jax.sharding import PartitionSpec as P

NX = 64
SHIFT = 3
MESH = pl.DeviceIdType.MESH

PLAN = (
    (
        (
            (0, 0, 1, 0), (0, 0, 0, 1), (0, 0, 0, 2), (0, 0, 0, 0), (0, 0, 1, 1), (0, 0, 1, 2),
        ),
        (
            (0, 1, 0, -1), (2, 0, 0, -1), (1, 0, 1, -1), (2, 0, 0, 0), (1, 0, 1, 1),
        ),
        (
            (0, 1, 0, 1), (0, 1, 1, -1), (2, 0, 1, -1), (1, 0, 0, -1), (0, 1, 1, 0),
        ),
        (
            (0, 1, 0, 0), (0, 1, 1, 1), (0, 2, 0, -1), (3, 0, 1, -1), (3, 0, 0, -1), (3, 0, 1, 2),
            (3, 0, 0, 2),
        ),
        (
            (0, 2, 0, 0), (0, 2, 0, 1), (0, 2, 1, -1), (2, 1, 0, -1), (1, 1, 1, -1),
        ),
        (
            (0, 2, 1, 0), (0, 2, 1, 1), (0, 3, 0, -1), (2, 1, 1, -1), (1, 1, 0, -1),
        ),
        (
            (2, 1, 0, 0), (1, 1, 1, 1), (0, 3, 1, -1), (2, 2, 0, -1), (1, 2, 0, -1),
        ),
        (
            (0, 3, 0, 0), (0, 3, 0, 1), (3, 2, 0, -1), (2, 2, 1, -1), (1, 2, 1, -1),
        ),
        (
            (0, 3, 1, 0), (0, 3, 1, 1), (3, 3, 1, -1), (3, 1, 1, -1), (3, 1, 0, -1),
        ),
        (
            (3, 2, 1, -1), (2, 3, 0, -1), (1, 3, 0, -1),
        ),
        (
            (3, 3, 0, -1), (2, 3, 1, -1), (1, 3, 1, -1),
        ),
    ),
    (
        (
            (0, 1, 1, 0), (0, 1, 0, 1), (0, 1, 0, 2), (0, 1, 0, 3), (0, 1, 0, 0), (0, 1, 1, 1),
            (0, 1, 1, 2), (0, 1, 1, 3),
        ),
        (
            (0, 0, 0, -1), (0, 2, 0, -1), (2, 1, 0, -1), (1, 1, 1, -1), (0, 0, 0, 0), (0, 2, 0, 1),
            (0, 0, 0, 2), (0, 2, 0, 3),
        ),
        (
            (0, 0, 0, 1), (0, 0, 1, -1), (0, 2, 1, -1), (2, 1, 1, -1), (1, 1, 0, -1), (0, 2, 1, 0),
            (0, 0, 1, 2), (0, 2, 1, 3),
        ),
        (
            (1, 1, 1, 1), (0, 3, 0, -1), (2, 2, 0, -1), (1, 0, 0, -1), (2, 2, 0, 0), (0, 3, 0, 3),
        ),
        (
            (0, 2, 0, 0), (0, 3, 1, -1), (2, 0, 0, -1), (1, 2, 1, -1), (1, 2, 1, 1), (0, 3, 1, 3),
            (3, 0, 1, -1), (3, 0, 1, 2),
        ),
        (
            (2, 1, 0, 0), (0, 0, 1, 1), (3, 1, 1, -1), (3, 2, 0, -1), (3, 2, 0, 3), (3, 0, 0, -1),
            (3, 0, 0, 2), (3, 3, 1, -1),
        ),
        (
            (0, 0, 1, 0), (0, 2, 1, 1), (3, 3, 1, 3), (3, 2, 1, -1), (1, 2, 0, -1), (3, 3, 0, -1),
        ),
        (
            (0, 3, 0, 0), (0, 3, 0, 1), (3, 2, 1, 3), (2, 0, 1, -1), (3, 1, 0, -1),
        ),
        (
            (0, 3, 1, 0), (0, 3, 1, 1), (3, 3, 0, 3), (2, 2, 1, -1), (1, 0, 1, -1),
        ),
        (
            (2, 3, 0, -1), (1, 3, 0, -1),
        ),
        (
            (2, 3, 1, -1), (1, 3, 1, -1),
        ),
    ),
)

GROUPS = (
    (
        ((0, 0), (0, 1), (2, 0), (1, 0)),
        ((3, 0), (0, 2), (2, 1), (1, 1)),
        ((0, 3), (2, 2), (1, 2), (3, 1)),
        ((3, 2), (2, 3), (1, 3), (3, 3)),
    ),
    (
        ((0, 1), (0, 0), (0, 2), (2, 1)),
        ((1, 1), (0, 3), (3, 0), (1, 2)),
        ((3, 2), (3, 3), (2, 0), (3, 1)),
        ((2, 2), (1, 0), (2, 3), (1, 3)),
    ),
)
UNITS = ((), (), ((0, 0),), ((0, 1),), (), (), ((1, 0),), ((1, 1),), ((2, 0),), ((2, 1),), ((3, 0), (3, 1)))
DEPTH = 1024
ROWS = 8


def kernel(
    orients, population,
    refs, parts, cid_in, oid_in, off_in, wts_in, out,
    rows, pv, turned, cid, oid, off, wts, top_s, tot_s, cho_s, part, recv1, send2, recv2,
    local_sem, ici_sem, sib_sem, send_sem, r1_sem, r2_sem, s1_sem, s2_sem,
):
    n_cls, n_ptl = part.shape[0], part.shape[1]
    voxels = refs.shape[2]
    half = pv.shape[1]
    cls, ptl = lax.axis_index("cls"), lax.axis_index("ptl")
    core, z = ptl % 2, ptl // 2
    far = z // 2
    sign = 1 - 2 * far
    place = z + far * (3 - 2 * z)
    along_x = cls + 1 - 2 * (cls % 2)
    along_y = cls + 2 - 4 * (cls // 2)
    column = (cls, along_x, along_y, 3 - cls)
    sibling = (cls, ptl + 1 - 2 * core)
    ways = (
        (along_x, ptl),
        (along_y, ptl),
        (cls, ptl + 2 * sign),
        (cls, ptl - 2 * sign),
    )

    def pair(q, zz):
        return column[q] * 4 + zz + far * (3 - 2 * zz)

    barrier = pltpu.get_barrier_semaphore()
    for q in (1, 2, 3):
        pl.semaphore_signal(barrier, inc=1, device_id=(column[q], ptl), device_id_type=MESH)
    for o in range(1, n_ptl):
        pl.semaphore_signal(
            barrier, inc=1, device_id=(cls, lax.rem(ptl + o, n_ptl)), device_id_type=MESH
        )
    loads = [
        pltpu.make_async_copy(parts.at[pl.ds(i * half, half)], pv.at[i], local_sem.at[i])
        for i in range(2)
    ]
    own = cls * 4 + z
    for h in range(2):
        loads.append(
            pltpu.make_async_copy(
                refs.at[0, pl.ds(16 * h, 16)], rows.at[own, core, h], local_sem.at[2 + h]
            )
        )
    for i, (a, b) in enumerate(((cid_in, cid), (oid_in, oid), (off_in, off), (wts_in, wts))):
        loads.append(pltpu.make_async_copy(a, b, local_sem.at[4 + i]))
    for load in loads:
        load.start()
    pl.semaphore_wait(barrier, 3 + n_ptl - 1)

    def send(src, p, h, way):
        target, recv, idx = (
            (sibling, sib_sem, 4) if way == 4 else (ways[way], ici_sem, way)
        )
        pltpu.make_async_remote_copy(
            src_ref=src,
            dst_ref=rows.at[p, core, h],
            send_sem=send_sem.at[idx],
            recv_sem=recv.at[p, h],
            device_id=target,
            device_id_type=MESH,
        ).start()

    def run(section, zc):
        for q, zz, h, way in section:
            p = pair(q, zz)
            block = rows.at[p, core, h]
            if way < 0:
                pltpu.make_async_copy(block, block, ici_sem.at[p, h]).wait()
                send(block, p, h, 4)
            elif q == 0 and zz == zc:
                send(refs.at[0, pl.ds(16 * h, 16)], p, h, way)
            else:
                send(block, p, h, way)

    top_s[...] = jnp.full(top_s.shape, -jnp.inf, jnp.float32)
    tot_s[...] = jnp.zeros(tot_s.shape, jnp.float32)
    cho_s[...] = jnp.zeros(cho_s.shape, jnp.float32)

    def scores(n, group):
        acc = jnp.zeros((len(group) * 64, half), jnp.float32)
        for k in range(0, voxels, DEPTH):
            lhs = jnp.concatenate(
                [rows[p, :, :, :, k : k + DEPTH].reshape(64, DEPTH) for p in group], axis=0
            )
            acc += lax.dot_general(
                lhs,
                turned[n, k : k + DEPTH, :],
                (((1,), (0,)), ((), ())),
                preferred_element_type=jnp.float32,
            )
        sc = acc * (1.0 / math.sqrt(voxels))
        cols = pl.ds(n * half, half)
        old = top_s[:, cols]
        new = jnp.maximum(old, jnp.max(sc, axis=0, keepdims=True))
        top_s[:, cols] = new
        tot_s[:, cols] = tot_s[:, cols] * jnp.exp(old - new) + jnp.sum(
            jnp.exp(sc - new), axis=0, keepdims=True
        )
        wanted = cid[:, cols] * orients + oid[:, cols]
        inner = lax.broadcasted_iota(jnp.int32, (64, half), 0)
        picked = jnp.zeros((1, half), jnp.float32)
        for i, p in enumerate(group):
            mine = inner == wanted - p * 64
            picked += jnp.sum(
                jnp.where(mine, sc[64 * i : 64 * i + 64], 0.0), axis=0, keepdims=True
            )
        cho_s[:, cols] += picked

    groups = [
        [jnp.where(place == 0, pair(*a), pair(*b)) for a, b in zip(first, second)]
        for first, second in zip(*GROUPS)
    ]
    for s, units in enumerate(UNITS):
        for zc in range(2):

            def branch(s=s, zc=zc):
                run(PLAN[zc][s], zc)
                if s == 0:
                    for h in range(2):
                        send(refs.at[0, pl.ds(16 * h, 16)], own, h, 4)

            pl.when(place == zc)(branch)
        if s == 0:
            for load in loads:
                load.wait()
        if s < 2:

            def turn(k, carry, n=s):
                span = pl.ds(pl.multiple_of(k * half, half), half)
                turned[n, span, :] = pv[n, :, span].T
                return carry

            lax.fori_loop(0, voxels // half, turn, 0)
        for g, n in units:
            if n == 0:
                for p in groups[g]:
                    for h in range(2):
                        block = rows.at[p, 1 - core, h]
                        pltpu.make_async_copy(block, block, sib_sem.at[p, h]).wait()
            scores(n, groups[g])

    gain = wts[...] * (n_cls * orients) * jnp.exp(cho_s[...] - top_s[...]) / tot_s[...]
    gain = gain.astype(jnp.bfloat16).astype(jnp.float32)
    code = (off[...] + SHIFT) * ROWS + cid[...]
    steps = 2 * SHIFT + 1
    which = lax.broadcasted_iota(jnp.int32, (steps * ROWS, 2 * half), 0)
    coef = jnp.where(which == code, gain, 0.0).astype(jnp.bfloat16)
    width = voxels // n_ptl
    lane = lax.broadcasted_iota(jnp.int32, (ROWS, 128), 1) % NX
    for j in range(n_ptl):
        pixels = pv[:, :, j * width : (j + 1) * width].reshape(2 * half, width)
        moved = jnp.dot(coef, pixels, preferred_element_type=jnp.float32)
        for v in range(width // 128):
            total = jnp.zeros((ROWS, 128), jnp.float32)
            for i, step in enumerate(range(-SHIFT, SHIFT + 1)):
                a = moved[i * ROWS : (i + 1) * ROWS, v * 128 : (v + 1) * 128]
                if step == 0:
                    total += a
                    continue
                inside = pltpu.roll(a, step % 128, 1)
                across = pltpu.roll(a, (step + NX) % 128, 1)
                keep = lane >= step if step > 0 else lane < NX + step
                total += jnp.where(keep, inside, across)
            for c in range(n_cls):
                part[c, j : j + 1, v * 128 : (v + 1) * 128] = total[c : c + 1]

    copies = []
    for q in (1, 2, 3):
        copies.append(
            pltpu.make_async_remote_copy(
                src_ref=part.at[column[q]],
                dst_ref=recv1.at[q - 1],
                send_sem=s1_sem.at[q - 1],
                recv_sem=r1_sem.at[q - 1],
                device_id=(column[q], ptl),
                device_id_type=MESH,
            )
        )
        copies[-1].start()
    for copy in copies:
        copy.wait_recv()
    mine = part[cls] + recv1[0] + recv1[1] + recv1[2]
    for j in range(n_ptl):
        send2[j] = mine[j : j + 1]
    for o in range(1, n_ptl):
        to = lax.rem(ptl + o, n_ptl)
        copies.append(
            pltpu.make_async_remote_copy(
                src_ref=send2.at[to],
                dst_ref=recv2.at[o - 1],
                send_sem=s2_sem.at[o - 1],
                recv_sem=r2_sem.at[o - 1],
                device_id=(cls, to),
                device_id_type=MESH,
            )
        )
        copies[-1].start()
    total = send2[ptl]
    for o in range(1, n_ptl):
        copies[2 + o].wait_recv()
        total += recv2[o - 1]
    out[...] = total / jnp.sqrt(jnp.float32(population))
    for copy in copies:
        copy.wait_send()

    def sent(count, idx):
        gone = rows.at[pl.ds(0, count), 0]
        pltpu.make_async_copy(gone, gone, send_sem.at[idx]).wait()

    sent(5, 0)
    sent(5, 1)
    sent(16, 4)

    @pl.when(place == 0)
    def _():
        sent(2, 2)

    @pl.when(place == 1)
    def _():
        sent(3, 2)
        sent(5, 3)


def fused(references, particles, class_ids, orient_ids, offsets, weights):
    n_cls = lax.axis_size("cls")
    n_ptl = lax.axis_size("ptl")
    _, local_ori, voxels = references.shape
    count = particles.shape[0]
    orients = local_ori * n_ptl
    population = count * n_ptl
    line = [x.reshape(1, count) for x in (class_ids, orient_ids, offsets, weights)]
    f32 = jnp.float32
    vmem = pl.BlockSpec(memory_space=pltpu.VMEM)
    hbm = pl.BlockSpec(memory_space=pl.ANY)
    return pl.pallas_call(
        functools.partial(kernel, orients, population),
        out_shape=jax.ShapeDtypeStruct((1, voxels // n_ptl), f32),
        in_specs=[hbm] * 6,
        out_specs=vmem,
        scratch_shapes=[
            pltpu.VMEM((n_cls * n_ptl // 2, 2, 2, local_ori // 2, voxels), references.dtype),
            pltpu.VMEM((2, count // 2, voxels), particles.dtype),
            pltpu.VMEM((2, voxels, count // 2), particles.dtype),
            *[pltpu.VMEM((1, count), x.dtype) for x in line],
            pltpu.VMEM((1, count), f32),
            pltpu.VMEM((1, count), f32),
            pltpu.VMEM((1, count), f32),
            pltpu.VMEM((n_cls, n_ptl, voxels // n_ptl), f32),
            pltpu.VMEM((n_cls - 1, n_ptl, voxels // n_ptl), f32),
            pltpu.VMEM((n_ptl, 1, voxels // n_ptl), f32),
            pltpu.VMEM((n_ptl - 1, 1, voxels // n_ptl), f32),
            pltpu.SemaphoreType.DMA((8,)),
            pltpu.SemaphoreType.DMA((n_cls * n_ptl // 2, 2)),
            pltpu.SemaphoreType.DMA((n_cls * n_ptl // 2, 2)),
            pltpu.SemaphoreType.DMA((5,)),
            pltpu.SemaphoreType.DMA((n_cls - 1,)),
            pltpu.SemaphoreType.DMA((n_ptl - 1,)),
            pltpu.SemaphoreType.DMA((n_cls - 1,)),
            pltpu.SemaphoreType.DMA((n_ptl - 1,)),
        ],
        compiler_params=pltpu.CompilerParams(
            collective_id=0, has_side_effects=True, vmem_limit_bytes=60 * 1024 * 1024
        ),
        cost_estimate=pl.CostEstimate(
            flops=2 * count * voxels * n_cls * orients,
            bytes_accessed=2 * voxels * (count + n_cls * orients),
            transcendentals=count * n_cls * orients,
        ),
    )(references, particles, *line)


def body(references, particles, class_ids, orient_ids, offsets, weights):
    n_cls = lax.axis_size("cls")
    n_ptl = lax.axis_size("ptl")
    per_owner, local_ori, voxels = references.shape
    orients = local_ori * n_ptl
    classes = per_owner * n_cls
    count = particles.shape[0]
    scale = 1.0 / math.sqrt(voxels)
    class_block = lax.all_gather(references, "ptl", axis=1, tiled=True)
    piece = lax.all_gather(class_block, "cls", axis=0, tiled=True)
    rows = piece.reshape(piece.shape[0] * orients, voxels)
    place = jnp.arange(rows.shape[0], dtype=jnp.int32)
    top = jnp.full((count,), -1e30, jnp.float32)
    scores = (
        lax.dot_general(
            particles, rows, (((1,), (1,)), ((), ())), preferred_element_type=jnp.float32
        )
        * scale
    )
    newtop = jnp.maximum(top, jnp.max(scores, axis=1))
    total = jnp.sum(jnp.exp(scores - newtop[:, None]), axis=1)
    picked = (class_ids[:, None] == (place // orients)[None, :]) & (
        orient_ids[:, None] == (place % orients)[None, :]
    )
    chosen = jnp.sum(jnp.where(picked, scores, 0.0), axis=1)
    top, total, chosen = (newtop, total, chosen)
    gain = (weights * (classes * orients) * jnp.exp(chosen - top) / total).astype(jnp.bfloat16)
    member = class_ids[None, :] == jnp.arange(classes, dtype=jnp.int32)[:, None]
    partial_sums = jnp.zeros((classes, voxels), jnp.float32)
    for step in range(-SHIFT, SHIFT + 1):
        coef = jnp.where(
            member & (offsets[None, :] == step), gain[None, :], jnp.zeros((), jnp.bfloat16)
        )
        moved = jnp.dot(coef, particles, preferred_element_type=jnp.float32)
        moved = jnp.roll(moved.reshape(classes, voxels // NX, NX), step, axis=2).reshape(
            classes, voxels
        )
        partial_sums = partial_sums + moved
    owned = lax.psum_scatter(partial_sums, "cls", scatter_dimension=0, tiled=True)
    owned = lax.psum_scatter(owned, "ptl", scatter_dimension=1, tiled=True)
    population = count * n_cls * n_ptl / classes
    return owned / jnp.sqrt(jnp.float32(population))


def solution(mesh):
    placed = (
        P("cls", "ptl", None),
        P(("cls", "ptl"), None),
        P(("cls", "ptl")),
        P(("cls", "ptl")),
        P(("cls", "ptl")),
        P(("cls", "ptl")),
    )
    planned = mesh.shape["cls"] == 4 and mesh.shape["ptl"] == 8
    return jax.shard_map(
        fused if planned else body,
        mesh=mesh,
        in_specs=placed,
        out_specs=P("cls", "ptl"),
        check_vma=False,
    )
```

```python
import functools
import math

import jax
import jax.numpy as jnp
from jax import lax
from jax.experimental import pallas as pl
from jax.experimental.pallas import tpu as pltpu
from jax.sharding import PartitionSpec as P

NX = 64
SHIFT = 3
MESH = pl.DeviceIdType.MESH

PLAN = (
    (
        (
            (0, 0, 1, 0), (0, 0, 0, 1), (0, 0, 0, 2), (0, 0, 0, 0), (0, 0, 1, 1), (0, 0, 1, 2),
        ),
        (
            (0, 1, 0, -1), (2, 0, 0, -1), (1, 0, 1, -1), (2, 0, 0, 0), (1, 0, 1, 1),
        ),
        (
            (0, 1, 1, -1), (2, 0, 1, -1), (1, 0, 0, -1), (0, 1, 1, 0), (0, 1, 0, 1),
        ),
        (
            (0, 2, 0, -1), (3, 0, 1, -1), (3, 0, 0, -1), (3, 0, 1, 2), (0, 1, 0, 0), (0, 1, 1, 1),
        ),
        (
            (3, 0, 0, 2), (0, 2, 1, -1), (2, 1, 0, -1), (1, 1, 1, -1), (0, 2, 0, 0), (0, 2, 0, 1),
        ),
        (
            (0, 3, 0, -1), (2, 1, 1, -1), (1, 1, 0, -1), (0, 2, 1, 0), (0, 2, 1, 1),
        ),
        (
            (0, 3, 1, -1), (2, 2, 0, -1), (1, 2, 0, -1), (2, 1, 0, 0), (1, 1, 1, 1),
        ),
        (
            (3, 2, 0, -1), (2, 2, 1, -1), (1, 2, 1, -1), (0, 3, 0, 0), (0, 3, 0, 1),
        ),
        (
            (3, 3, 1, -1), (3, 1, 1, -1), (3, 1, 0, -1), (0, 3, 1, 0), (0, 3, 1, 1),
        ),
        (
            (3, 2, 1, -1), (2, 3, 0, -1), (1, 3, 0, -1),
        ),
        (
            (3, 3, 0, -1), (2, 3, 1, -1), (1, 3, 1, -1),
        ),
    ),
    (
        (
            (0, 1, 1, 0), (0, 1, 0, 1), (0, 1, 0, 2), (0, 1, 0, 3), (0, 1, 0, 0), (0, 1, 1, 1),
            (0, 1, 1, 2), (0, 1, 1, 3),
        ),
        (
            (0, 0, 0, -1), (0, 2, 0, -1), (2, 1, 0, -1), (1, 1, 1, -1), (0, 0, 0, 0), (0, 2, 0, 1),
            (0, 0, 0, 2), (0, 2, 0, 3),
        ),
        (
            (0, 0, 1, -1), (0, 2, 1, -1), (2, 1, 1, -1), (1, 1, 0, -1), (0, 2, 1, 0), (0, 0, 0, 1),
            (0, 0, 1, 2), (0, 2, 1, 3),
        ),
        (
            (0, 3, 0, -1), (2, 2, 0, -1), (1, 0, 0, -1), (2, 2, 0, 0), (1, 1, 1, 1), (0, 3, 0, 3),
        ),
        (
            (0, 3, 1, -1), (2, 0, 0, -1), (1, 2, 1, -1), (0, 2, 0, 0), (1, 2, 1, 1), (0, 3, 1, 3),
            (3, 0, 1, -1), (3, 0, 1, 2),
        ),
        (
            (3, 1, 1, -1), (3, 2, 0, -1), (2, 1, 0, 0), (0, 0, 1, 1), (3, 2, 0, 3), (3, 0, 0, -1),
            (3, 0, 0, 2),
        ),
        (
            (3, 3, 1, -1), (3, 2, 1, -1), (1, 2, 0, -1), (0, 0, 1, 0), (0, 2, 1, 1), (3, 3, 1, 3),
        ),
        (
            (3, 3, 0, -1), (2, 0, 1, -1), (3, 1, 0, -1), (0, 3, 0, 0), (0, 3, 0, 1), (3, 2, 1, 3),
        ),
        (
            (2, 2, 1, -1), (1, 0, 1, -1), (0, 3, 1, 0), (0, 3, 1, 1), (3, 3, 0, 3),
        ),
        (
            (2, 3, 0, -1), (1, 3, 0, -1),
        ),
        (
            (2, 3, 1, -1), (1, 3, 1, -1),
        ),
    ),
)

GROUPS = (
    (
        ((0, 0), (0, 1), (2, 0), (1, 0)),
        ((3, 0), (0, 2), (2, 1), (1, 1)),
        ((0, 3), (2, 2), (1, 2), (3, 1)),
        ((3, 2), (3, 3), (2, 3), (1, 3)),
    ),
    (
        ((0, 1), (0, 0), (0, 2), (2, 1)),
        ((1, 1), (0, 3), (3, 0), (1, 2)),
        ((3, 2), (2, 0), (3, 1), (3, 3)),
        ((2, 2), (1, 0), (2, 3), (1, 3)),
    ),
)
UNITS = ((), (), ((0, 0),), ((0, 1),), (), (), ((1, 0),), ((1, 1),), ((2, 0),), ((2, 1),), ((3, 0), (3, 1)))
DEPTH = 1024
ROWS = 8


def kernel(
    orients, population,
    refs, parts, cid_in, oid_in, off_in, wts_in, out,
    rows, pv, cid, oid, off, wts, top_s, tot_s, cho_s, part, recv1, send2, recv2,
    local_sem, ici_sem, sib_sem, send_sem, r1_sem, r2_sem, s1_sem, s2_sem,
):
    n_cls, n_ptl = part.shape[0], part.shape[1]
    voxels = refs.shape[2]
    half = pv.shape[1]
    cls, ptl = lax.axis_index("cls"), lax.axis_index("ptl")
    core, z = ptl % 2, ptl // 2
    far = z // 2
    sign = 1 - 2 * far
    place = z + far * (3 - 2 * z)
    along_x = cls + 1 - 2 * (cls % 2)
    along_y = cls + 2 - 4 * (cls // 2)
    column = (cls, along_x, along_y, 3 - cls)
    sibling = (cls, ptl + 1 - 2 * core)
    ways = (
        (along_x, ptl),
        (along_y, ptl),
        (cls, ptl + 2 * sign),
        (cls, ptl - 2 * sign),
    )

    def pair(q, zz):
        return column[q] * 4 + zz + far * (3 - 2 * zz)

    barrier = pltpu.get_barrier_semaphore()
    for q in (1, 2, 3):
        pl.semaphore_signal(barrier, inc=1, device_id=(column[q], ptl), device_id_type=MESH)
    for o in range(1, n_ptl):
        pl.semaphore_signal(
            barrier, inc=1, device_id=(cls, lax.rem(ptl + o, n_ptl)), device_id_type=MESH
        )
    loads = [
        pltpu.make_async_copy(parts.at[pl.ds(i * half, half)], pv.at[i], local_sem.at[i])
        for i in range(2)
    ]
    own = cls * 4 + z
    for h in range(2):
        loads.append(
            pltpu.make_async_copy(
                refs.at[0, pl.ds(16 * h, 16)], rows.at[own, core, h], local_sem.at[2 + h]
            )
        )
    for i, (a, b) in enumerate(((cid_in, cid), (oid_in, oid), (off_in, off), (wts_in, wts))):
        loads.append(pltpu.make_async_copy(a, b, local_sem.at[4 + i]))
    for load in loads:
        load.start()
    pl.semaphore_wait(barrier, 3 + n_ptl - 1)

    def send(src, p, h, way):
        target, recv, idx = (
            (sibling, sib_sem, 4) if way == 4 else (ways[way], ici_sem, way)
        )
        pltpu.make_async_remote_copy(
            src_ref=src,
            dst_ref=rows.at[p, core, h],
            send_sem=send_sem.at[idx],
            recv_sem=recv.at[p, h],
            device_id=target,
            device_id_type=MESH,
        ).start()

    def run(section, zc):
        for q, zz, h, way in section:
            p = pair(q, zz)
            block = rows.at[p, core, h]
            if way < 0:
                pltpu.make_async_copy(block, block, ici_sem.at[p, h]).wait()
                send(block, p, h, 4)
            elif q == 0 and zz == zc:
                send(refs.at[0, pl.ds(16 * h, 16)], p, h, way)
            else:
                send(block, p, h, way)

    top_s[...] = jnp.full(top_s.shape, -jnp.inf, jnp.float32)
    tot_s[...] = jnp.zeros(tot_s.shape, jnp.float32)
    cho_s[...] = jnp.zeros(cho_s.shape, jnp.float32)

    def scores(n, group):
        acc = jnp.zeros((len(group) * 64, half), jnp.float32)
        for k in range(0, voxels, DEPTH):
            lhs = jnp.concatenate(
                [rows[p, :, :, :, k : k + DEPTH].reshape(64, DEPTH) for p in group], axis=0
            )
            acc += lax.dot_general(
                lhs,
                pv[n, :, k : k + DEPTH],
                (((1,), (1,)), ((), ())),
                preferred_element_type=jnp.float32,
            )
        sc = acc * (1.0 / math.sqrt(voxels))
        cols = pl.ds(n * half, half)
        old = top_s[:, cols]
        new = jnp.maximum(old, jnp.max(sc, axis=0, keepdims=True))
        top_s[:, cols] = new
        tot_s[:, cols] = tot_s[:, cols] * jnp.exp(old - new) + jnp.sum(
            jnp.exp(sc - new), axis=0, keepdims=True
        )
        wanted = cid[:, cols] * orients + oid[:, cols]
        inner = lax.broadcasted_iota(jnp.int32, (64, half), 0)
        picked = jnp.zeros((1, half), jnp.float32)
        for i, p in enumerate(group):
            mine = inner == wanted - p * 64
            picked += jnp.sum(
                jnp.where(mine, sc[64 * i : 64 * i + 64], 0.0), axis=0, keepdims=True
            )
        cho_s[:, cols] += picked

    groups = [
        [jnp.where(place == 0, pair(*a), pair(*b)) for a, b in zip(first, second)]
        for first, second in zip(*GROUPS)
    ]
    for s, units in enumerate(UNITS):
        for zc in range(2):

            def branch(s=s, zc=zc):
                run(PLAN[zc][s], zc)
                if s == 0:
                    for h in range(2):
                        send(refs.at[0, pl.ds(16 * h, 16)], own, h, 4)

            pl.when(place == zc)(branch)
        if s == 0:
            for load in loads:
                load.wait()
        for g, n in units:
            if n == 0:
                for p in groups[g]:
                    for h in range(2):
                        block = rows.at[p, 1 - core, h]
                        pltpu.make_async_copy(block, block, sib_sem.at[p, h]).wait()
            scores(n, groups[g])

    gain = wts[...] * (n_cls * orients) * jnp.exp(cho_s[...] - top_s[...]) / tot_s[...]
    gain = gain.astype(jnp.bfloat16).astype(jnp.float32)
    code = (off[...] + SHIFT) * ROWS + cid[...]
    steps = 2 * SHIFT + 1
    which = lax.broadcasted_iota(jnp.int32, (steps * ROWS, 2 * half), 0)
    coef = jnp.where(which == code, gain, 0.0).astype(jnp.bfloat16)
    width = voxels // n_ptl
    lane = lax.broadcasted_iota(jnp.int32, (ROWS, 128), 1) % NX
    for j in range(n_ptl):
        pixels = pv[:, :, j * width : (j + 1) * width].reshape(2 * half, width)
        moved = jnp.dot(coef, pixels, preferred_element_type=jnp.float32)
        for v in range(width // 128):
            total = jnp.zeros((ROWS, 128), jnp.float32)
            for i, step in enumerate(range(-SHIFT, SHIFT + 1)):
                a = moved[i * ROWS : (i + 1) * ROWS, v * 128 : (v + 1) * 128]
                if step == 0:
                    total += a
                    continue
                inside = pltpu.roll(a, step % 128, 1)
                across = pltpu.roll(a, (step + NX) % 128, 1)
                keep = lane >= step if step > 0 else lane < NX + step
                total += jnp.where(keep, inside, across)
            for c in range(n_cls):
                part[c, j : j + 1, v * 128 : (v + 1) * 128] = total[c : c + 1]

    copies = []
    for q in (1, 2, 3):
        copies.append(
            pltpu.make_async_remote_copy(
                src_ref=part.at[column[q]],
                dst_ref=recv1.at[q - 1],
                send_sem=s1_sem.at[q - 1],
                recv_sem=r1_sem.at[q - 1],
                device_id=(column[q], ptl),
                device_id_type=MESH,
            )
        )
        copies[-1].start()
    for copy in copies:
        copy.wait_recv()
    mine = part[cls] + recv1[0] + recv1[1] + recv1[2]
    for j in range(n_ptl):
        send2[j] = mine[j : j + 1]
    for o in range(1, n_ptl):
        to = lax.rem(ptl + o, n_ptl)
        copies.append(
            pltpu.make_async_remote_copy(
                src_ref=send2.at[to],
                dst_ref=recv2.at[o - 1],
                send_sem=s2_sem.at[o - 1],
                recv_sem=r2_sem.at[o - 1],
                device_id=(cls, to),
                device_id_type=MESH,
            )
        )
        copies[-1].start()
    total = send2[ptl]
    for o in range(1, n_ptl):
        copies[2 + o].wait_recv()
        total += recv2[o - 1]
    out[...] = total / jnp.sqrt(jnp.float32(population))
    for copy in copies:
        copy.wait_send()

    def sent(count, idx):
        gone = rows.at[pl.ds(0, count), 0]
        pltpu.make_async_copy(gone, gone, send_sem.at[idx]).wait()

    sent(5, 0)
    sent(5, 1)
    sent(16, 4)

    @pl.when(place == 0)
    def _():
        sent(2, 2)

    @pl.when(place == 1)
    def _():
        sent(3, 2)
        sent(5, 3)


def fused(references, particles, class_ids, orient_ids, offsets, weights):
    n_cls = lax.axis_size("cls")
    n_ptl = lax.axis_size("ptl")
    _, local_ori, voxels = references.shape
    count = particles.shape[0]
    orients = local_ori * n_ptl
    population = count * n_ptl
    line = [x.reshape(1, count) for x in (class_ids, orient_ids, offsets, weights)]
    f32 = jnp.float32
    vmem = pl.BlockSpec(memory_space=pltpu.VMEM)
    hbm = pl.BlockSpec(memory_space=pl.ANY)
    return pl.pallas_call(
        functools.partial(kernel, orients, population),
        out_shape=jax.ShapeDtypeStruct((1, voxels // n_ptl), f32),
        in_specs=[hbm] * 6,
        out_specs=vmem,
        scratch_shapes=[
            pltpu.VMEM((n_cls * n_ptl // 2, 2, 2, local_ori // 2, voxels), references.dtype),
            pltpu.VMEM((2, count // 2, voxels), particles.dtype),
            *[pltpu.VMEM((1, count), x.dtype) for x in line],
            pltpu.VMEM((1, count), f32),
            pltpu.VMEM((1, count), f32),
            pltpu.VMEM((1, count), f32),
            pltpu.VMEM((n_cls, n_ptl, voxels // n_ptl), f32),
            pltpu.VMEM((n_cls - 1, n_ptl, voxels // n_ptl), f32),
            pltpu.VMEM((n_ptl, 1, voxels // n_ptl), f32),
            pltpu.VMEM((n_ptl - 1, 1, voxels // n_ptl), f32),
            pltpu.SemaphoreType.DMA((8,)),
            pltpu.SemaphoreType.DMA((n_cls * n_ptl // 2, 2)),
            pltpu.SemaphoreType.DMA((n_cls * n_ptl // 2, 2)),
            pltpu.SemaphoreType.DMA((5,)),
            pltpu.SemaphoreType.DMA((n_cls - 1,)),
            pltpu.SemaphoreType.DMA((n_ptl - 1,)),
            pltpu.SemaphoreType.DMA((n_cls - 1,)),
            pltpu.SemaphoreType.DMA((n_ptl - 1,)),
        ],
        compiler_params=pltpu.CompilerParams(
            collective_id=0, has_side_effects=True, vmem_limit_bytes=60 * 1024 * 1024
        ),
        cost_estimate=pl.CostEstimate(
            flops=2 * count * voxels * n_cls * orients,
            bytes_accessed=2 * voxels * (count + n_cls * orients),
            transcendentals=count * n_cls * orients,
        ),
    )(references, particles, *line)


def body(references, particles, class_ids, orient_ids, offsets, weights):
    n_cls = lax.axis_size("cls")
    n_ptl = lax.axis_size("ptl")
    per_owner, local_ori, voxels = references.shape
    orients = local_ori * n_ptl
    classes = per_owner * n_cls
    count = particles.shape[0]
    scale = 1.0 / math.sqrt(voxels)
    class_block = lax.all_gather(references, "ptl", axis=1, tiled=True)
    piece = lax.all_gather(class_block, "cls", axis=0, tiled=True)
    rows = piece.reshape(piece.shape[0] * orients, voxels)
    place = jnp.arange(rows.shape[0], dtype=jnp.int32)
    top = jnp.full((count,), -1e30, jnp.float32)
    scores = (
        lax.dot_general(
            particles, rows, (((1,), (1,)), ((), ())), preferred_element_type=jnp.float32
        )
        * scale
    )
    newtop = jnp.maximum(top, jnp.max(scores, axis=1))
    total = jnp.sum(jnp.exp(scores - newtop[:, None]), axis=1)
    picked = (class_ids[:, None] == (place // orients)[None, :]) & (
        orient_ids[:, None] == (place % orients)[None, :]
    )
    chosen = jnp.sum(jnp.where(picked, scores, 0.0), axis=1)
    top, total, chosen = (newtop, total, chosen)
    gain = (weights * (classes * orients) * jnp.exp(chosen - top) / total).astype(jnp.bfloat16)
    member = class_ids[None, :] == jnp.arange(classes, dtype=jnp.int32)[:, None]
    partial_sums = jnp.zeros((classes, voxels), jnp.float32)
    for step in range(-SHIFT, SHIFT + 1):
        coef = jnp.where(
            member & (offsets[None, :] == step), gain[None, :], jnp.zeros((), jnp.bfloat16)
        )
        moved = jnp.dot(coef, particles, preferred_element_type=jnp.float32)
        moved = jnp.roll(moved.reshape(classes, voxels // NX, NX), step, axis=2).reshape(
            classes, voxels
        )
        partial_sums = partial_sums + moved
    owned = lax.psum_scatter(partial_sums, "cls", scatter_dimension=0, tiled=True)
    owned = lax.psum_scatter(owned, "ptl", scatter_dimension=1, tiled=True)
    population = count * n_cls * n_ptl / classes
    return owned / jnp.sqrt(jnp.float32(population))


def solution(mesh):
    placed = (
        P("cls", "ptl", None),
        P(("cls", "ptl"), None),
        P(("cls", "ptl")),
        P(("cls", "ptl")),
        P(("cls", "ptl")),
        P(("cls", "ptl")),
    )
    planned = mesh.shape["cls"] == 4 and mesh.shape["ptl"] == 8
    return jax.shard_map(
        fused if planned else body,
        mesh=mesh,
        in_specs=placed,
        out_specs=P("cls", "ptl"),
        check_vma=False,
    )
```

```python
import functools
import math

import jax
import jax.numpy as jnp
from jax import lax
from jax.experimental import pallas as pl
from jax.experimental.pallas import tpu as pltpu
from jax.sharding import PartitionSpec as P

NX = 64
SHIFT = 3
MESH = pl.DeviceIdType.MESH

PLAN = (
    (
        (
            (0, 0, 1, 0), (0, 0, 0, 1), (0, 0, 0, 2), (0, 0, 0, 0), (0, 0, 1, 1), (0, 0, 1, 2),
        ),
        (
            (0, 1, 0, -1), (2, 0, 0, -1), (1, 0, 1, -1), (2, 0, 0, 0), (1, 0, 1, 1),
        ),
        (
            (0, 1, 0, 1), (0, 1, 1, -1), (2, 0, 1, -1), (1, 0, 0, -1), (0, 1, 1, 0),
        ),
        (
            (0, 1, 0, 0), (0, 1, 1, 1), (0, 2, 0, -1), (3, 0, 1, -1), (3, 0, 0, -1), (3, 0, 1, 2),
            (3, 0, 0, 2),
        ),
        (
            (0, 2, 0, 0), (0, 2, 0, 1), (0, 2, 1, -1), (2, 1, 0, -1), (1, 1, 1, -1),
        ),
        (
            (0, 2, 1, 0), (0, 2, 1, 1), (0, 3, 0, -1), (2, 1, 1, -1), (1, 1, 0, -1),
        ),
        (
            (2, 1, 0, 0), (1, 1, 1, 1), (0, 3, 1, -1), (2, 2, 0, -1), (1, 2, 0, -1),
        ),
        (
            (0, 3, 0, 0), (0, 3, 0, 1), (3, 2, 0, -1), (2, 2, 1, -1), (1, 2, 1, -1),
        ),
        (
            (0, 3, 1, 0), (0, 3, 1, 1), (3, 3, 1, -1), (3, 1, 1, -1), (3, 1, 0, -1),
        ),
        (
            (3, 2, 1, -1), (2, 3, 0, -1), (1, 3, 0, -1),
        ),
        (
            (3, 3, 0, -1), (2, 3, 1, -1), (1, 3, 1, -1),
        ),
    ),
    (
        (
            (0, 1, 1, 0), (0, 1, 0, 1), (0, 1, 0, 2), (0, 1, 0, 3), (0, 1, 0, 0), (0, 1, 1, 1),
            (0, 1, 1, 2), (0, 1, 1, 3),
        ),
        (
            (0, 0, 0, -1), (0, 2, 0, -1), (2, 1, 0, -1), (1, 1, 1, -1), (0, 0, 0, 0), (0, 2, 0, 1),
            (0, 0, 0, 2), (0, 2, 0, 3),
        ),
        (
            (0, 0, 0, 1), (0, 0, 1, -1), (0, 2, 1, -1), (2, 1, 1, -1), (1, 1, 0, -1), (0, 2, 1, 0),
            (0, 0, 1, 2), (0, 2, 1, 3),
        ),
        (
            (1, 1, 1, 1), (0, 3, 0, -1), (2, 2, 0, -1), (1, 0, 0, -1), (2, 2, 0, 0), (0, 3, 0, 3),
        ),
        (
            (0, 2, 0, 0), (0, 3, 1, -1), (2, 0, 0, -1), (1, 2, 1, -1), (1, 2, 1, 1), (0, 3, 1, 3),
            (3, 0, 1, -1), (3, 0, 1, 2),
        ),
        (
            (2, 1, 0, 0), (0, 0, 1, 1), (3, 1, 1, -1), (3, 2, 0, -1), (3, 2, 0, 3), (3, 0, 0, -1),
            (3, 0, 0, 2), (3, 3, 1, -1),
        ),
        (
            (0, 0, 1, 0), (0, 2, 1, 1), (3, 3, 1, 3), (3, 2, 1, -1), (1, 2, 0, -1), (3, 3, 0, -1),
        ),
        (
            (0, 3, 0, 0), (0, 3, 0, 1), (3, 2, 1, 3), (2, 0, 1, -1), (3, 1, 0, -1),
        ),
        (
            (0, 3, 1, 0), (0, 3, 1, 1), (3, 3, 0, 3), (2, 2, 1, -1), (1, 0, 1, -1),
        ),
        (
            (2, 3, 0, -1), (1, 3, 0, -1),
        ),
        (
            (2, 3, 1, -1), (1, 3, 1, -1),
        ),
    ),
)

GROUPS = (
    (
        ((0, 0), (0, 1), (2, 0), (1, 0)),
        ((3, 0), (0, 2), (2, 1), (1, 1)),
        ((0, 3), (2, 2), (1, 2), (3, 1)),
        ((3, 2), (2, 3), (1, 3), (3, 3)),
    ),
    (
        ((0, 1), (0, 0), (0, 2), (2, 1)),
        ((1, 1), (0, 3), (3, 0), (1, 2)),
        ((3, 2), (3, 3), (2, 0), (3, 1)),
        ((2, 2), (1, 0), (2, 3), (1, 3)),
    ),
)
UNITS = ((), (), ((0, 0),), ((0, 1),), (), (), ((1, 0),), ((1, 1),), ((2, 0),), ((2, 1),), ((3, 0), (3, 1)))
DEPTH = 1024
ROWS = 8


def kernel(
    orients, population,
    refs, parts, cid_in, oid_in, off_in, wts_in, out,
    rows, pv, cid, oid, off, wts, top_s, tot_s, cho_s, part, recv1, send2, recv2,
    local_sem, ici_sem, sib_sem, send_sem, r1_sem, r2_sem, s1_sem, s2_sem,
):
    n_ptl, n_cls = part.shape[0], part.shape[1]
    voxels = refs.shape[2]
    half = pv.shape[1]
    cls, ptl = lax.axis_index("cls"), lax.axis_index("ptl")
    core, z = ptl % 2, ptl // 2
    far = z // 2
    sign = 1 - 2 * far
    place = z + far * (3 - 2 * z)
    along_x = cls + 1 - 2 * (cls % 2)
    along_y = cls + 2 - 4 * (cls // 2)
    column = (cls, along_x, along_y, 3 - cls)
    sibling = (cls, ptl + 1 - 2 * core)
    ways = (
        (along_x, ptl),
        (along_y, ptl),
        (cls, ptl + 2 * sign),
        (cls, ptl - 2 * sign),
    )

    def pair(q, zz):
        return column[q] * 4 + zz + far * (3 - 2 * zz)

    barrier = pltpu.get_barrier_semaphore()
    for q in (1, 2, 3):
        pl.semaphore_signal(barrier, inc=1, device_id=(column[q], ptl), device_id_type=MESH)
    for o in range(1, n_ptl):
        pl.semaphore_signal(
            barrier, inc=1, device_id=(cls, lax.rem(ptl + o, n_ptl)), device_id_type=MESH
        )
    loads = [
        pltpu.make_async_copy(parts.at[pl.ds(i * half, half)], pv.at[i], local_sem.at[i])
        for i in range(2)
    ]
    own = cls * 4 + z
    for h in range(2):
        loads.append(
            pltpu.make_async_copy(
                refs.at[0, pl.ds(16 * h, 16)], rows.at[own, core, h], local_sem.at[2 + h]
            )
        )
    for i, (a, b) in enumerate(((cid_in, cid), (oid_in, oid), (off_in, off), (wts_in, wts))):
        loads.append(pltpu.make_async_copy(a, b, local_sem.at[4 + i]))
    for load in loads:
        load.start()
    pl.semaphore_wait(barrier, 3 + n_ptl - 1)

    def send(src, p, h, way):
        target, recv, idx = (
            (sibling, sib_sem, 4) if way == 4 else (ways[way], ici_sem, way)
        )
        pltpu.make_async_remote_copy(
            src_ref=src,
            dst_ref=rows.at[p, core, h],
            send_sem=send_sem.at[idx],
            recv_sem=recv.at[p, h],
            device_id=target,
            device_id_type=MESH,
        ).start()

    def run(section, zc):
        for q, zz, h, way in section:
            p = pair(q, zz)
            block = rows.at[p, core, h]
            if way < 0:
                pltpu.make_async_copy(block, block, ici_sem.at[p, h]).wait()
                send(block, p, h, 4)
            elif q == 0 and zz == zc:
                send(refs.at[0, pl.ds(16 * h, 16)], p, h, way)
            else:
                send(block, p, h, way)

    top_s[...] = jnp.full(top_s.shape, -jnp.inf, jnp.float32)
    tot_s[...] = jnp.zeros(tot_s.shape, jnp.float32)
    cho_s[...] = jnp.zeros(cho_s.shape, jnp.float32)

    def scores(n, group):
        acc = jnp.zeros((len(group) * 64, half), jnp.float32)
        for k in range(0, voxels, DEPTH):
            lhs = jnp.concatenate(
                [rows[p, :, :, :, k : k + DEPTH].reshape(64, DEPTH) for p in group], axis=0
            )
            acc += lax.dot_general(
                lhs,
                pv[n, :, k : k + DEPTH],
                (((1,), (1,)), ((), ())),
                preferred_element_type=jnp.float32,
            )
        sc = acc * (1.0 / math.sqrt(voxels))
        cols = pl.ds(n * half, half)
        old = top_s[:, cols]
        new = jnp.maximum(old, jnp.max(sc, axis=0, keepdims=True))
        top_s[:, cols] = new
        tot_s[:, cols] = tot_s[:, cols] * jnp.exp(old - new) + jnp.sum(
            jnp.exp(sc - new), axis=0, keepdims=True
        )
        wanted = cid[:, cols] * orients + oid[:, cols]
        inner = lax.broadcasted_iota(jnp.int32, (64, half), 0)
        picked = jnp.zeros((1, half), jnp.float32)
        for i, p in enumerate(group):
            mine = inner == wanted - p * 64
            picked += jnp.sum(
                jnp.where(mine, sc[64 * i : 64 * i + 64], 0.0), axis=0, keepdims=True
            )
        cho_s[:, cols] += picked

    groups = [
        [jnp.where(place == 0, pair(*a), pair(*b)) for a, b in zip(first, second)]
        for first, second in zip(*GROUPS)
    ]
    for s, units in enumerate(UNITS):
        for zc in range(2):

            def branch(s=s, zc=zc):
                run(PLAN[zc][s], zc)
                if s == 0:
                    for h in range(2):
                        send(refs.at[0, pl.ds(16 * h, 16)], own, h, 4)

            pl.when(place == zc)(branch)
        if s == 0:
            for load in loads:
                load.wait()
        for g, n in units:
            if n == 0:
                for p in groups[g]:
                    for h in range(2):
                        block = rows.at[p, 1 - core, h]
                        pltpu.make_async_copy(block, block, sib_sem.at[p, h]).wait()
            scores(n, groups[g])

    gain = wts[...] * (n_cls * orients) * jnp.exp(cho_s[...] - top_s[...]) / tot_s[...]
    gain = gain.astype(jnp.bfloat16).astype(jnp.float32)
    code = (off[...] + SHIFT) * ROWS + cid[...]
    steps = 2 * SHIFT + 1
    which = lax.broadcasted_iota(jnp.int32, (steps * ROWS, 2 * half), 0)
    coef = jnp.where(which == code, gain, 0.0).astype(jnp.bfloat16)
    width = voxels // n_ptl
    lane = lax.broadcasted_iota(jnp.int32, (ROWS, 128), 1) % NX
    copies = []
    for o in range(1, n_ptl + 1):
        owner = lax.rem(ptl + o, n_ptl)
        columns = pl.ds(pl.multiple_of(owner * width, width), width)
        pixels = pv[:, :, columns].reshape(2 * half, width)
        moved = jnp.dot(coef, pixels, preferred_element_type=jnp.float32)
        for v in range(width // 128):
            total = jnp.zeros((ROWS, 128), jnp.float32)
            for i, step in enumerate(range(-SHIFT, SHIFT + 1)):
                a = moved[i * ROWS : (i + 1) * ROWS, v * 128 : (v + 1) * 128]
                if step == 0:
                    total += a
                    continue
                inside = pltpu.roll(a, step % 128, 1)
                across = pltpu.roll(a, (step + NX) % 128, 1)
                keep = lane >= step if step > 0 else lane < NX + step
                total += jnp.where(keep, inside, across)
            part[o - 1, :, v * 128 : (v + 1) * 128] = total[:n_cls]
        if o < n_ptl:
            copies.append(
                pltpu.make_async_remote_copy(
                    src_ref=part.at[o - 1],
                    dst_ref=recv1.at[o - 1],
                    send_sem=s1_sem.at[o - 1],
                    recv_sem=r1_sem.at[o - 1],
                    device_id=(cls, owner),
                    device_id_type=MESH,
                )
            )
            copies[-1].start()
    mine = part[n_ptl - 1]
    for o in range(1, n_ptl):
        copies[o - 1].wait_recv()
        mine += recv1[o - 1]
    for c in range(n_cls):
        send2[c] = mine[c : c + 1]
    last = []
    for q in (1, 2, 3):
        last.append(
            pltpu.make_async_remote_copy(
                src_ref=send2.at[column[q]],
                dst_ref=recv2.at[q - 1],
                send_sem=s2_sem.at[q - 1],
                recv_sem=r2_sem.at[q - 1],
                device_id=(column[q], ptl),
                device_id_type=MESH,
            )
        )
        last[-1].start()
    total = send2[cls]
    for q in (1, 2, 3):
        last[q - 1].wait_recv()
        total += recv2[q - 1]
    out[...] = total / jnp.sqrt(jnp.float32(population))
    for copy in copies + last:
        copy.wait_send()

    def sent(count, idx):
        gone = rows.at[pl.ds(0, count), 0]
        pltpu.make_async_copy(gone, gone, send_sem.at[idx]).wait()

    sent(5, 0)
    sent(5, 1)
    sent(16, 4)

    @pl.when(place == 0)
    def _():
        sent(2, 2)

    @pl.when(place == 1)
    def _():
        sent(3, 2)
        sent(5, 3)


def fused(references, particles, class_ids, orient_ids, offsets, weights):
    n_cls = lax.axis_size("cls")
    n_ptl = lax.axis_size("ptl")
    _, local_ori, voxels = references.shape
    count = particles.shape[0]
    orients = local_ori * n_ptl
    population = count * n_ptl
    line = [x.reshape(1, count) for x in (class_ids, orient_ids, offsets, weights)]
    f32 = jnp.float32
    vmem = pl.BlockSpec(memory_space=pltpu.VMEM)
    hbm = pl.BlockSpec(memory_space=pl.ANY)
    return pl.pallas_call(
        functools.partial(kernel, orients, population),
        out_shape=jax.ShapeDtypeStruct((1, voxels // n_ptl), f32),
        in_specs=[hbm] * 6,
        out_specs=vmem,
        scratch_shapes=[
            pltpu.VMEM((n_cls * n_ptl // 2, 2, 2, local_ori // 2, voxels), references.dtype),
            pltpu.VMEM((2, count // 2, voxels), particles.dtype),
            *[pltpu.VMEM((1, count), x.dtype) for x in line],
            pltpu.VMEM((1, count), f32),
            pltpu.VMEM((1, count), f32),
            pltpu.VMEM((1, count), f32),
            pltpu.VMEM((n_ptl, n_cls, voxels // n_ptl), f32),
            pltpu.VMEM((n_ptl - 1, n_cls, voxels // n_ptl), f32),
            pltpu.VMEM((n_cls, 1, voxels // n_ptl), f32),
            pltpu.VMEM((n_cls - 1, 1, voxels // n_ptl), f32),
            pltpu.SemaphoreType.DMA((8,)),
            pltpu.SemaphoreType.DMA((n_cls * n_ptl // 2, 2)),
            pltpu.SemaphoreType.DMA((n_cls * n_ptl // 2, 2)),
            pltpu.SemaphoreType.DMA((5,)),
            pltpu.SemaphoreType.DMA((n_ptl - 1,)),
            pltpu.SemaphoreType.DMA((n_cls - 1,)),
            pltpu.SemaphoreType.DMA((n_ptl - 1,)),
            pltpu.SemaphoreType.DMA((n_cls - 1,)),
        ],
        compiler_params=pltpu.CompilerParams(
            collective_id=0, has_side_effects=True, vmem_limit_bytes=60 * 1024 * 1024
        ),
        cost_estimate=pl.CostEstimate(
            flops=2 * count * voxels * n_cls * orients,
            bytes_accessed=2 * voxels * (count + n_cls * orients),
            transcendentals=count * n_cls * orients,
        ),
    )(references, particles, *line)


def body(references, particles, class_ids, orient_ids, offsets, weights):
    n_cls = lax.axis_size("cls")
    n_ptl = lax.axis_size("ptl")
    per_owner, local_ori, voxels = references.shape
    orients = local_ori * n_ptl
    classes = per_owner * n_cls
    count = particles.shape[0]
    scale = 1.0 / math.sqrt(voxels)
    class_block = lax.all_gather(references, "ptl", axis=1, tiled=True)
    piece = lax.all_gather(class_block, "cls", axis=0, tiled=True)
    rows = piece.reshape(piece.shape[0] * orients, voxels)
    place = jnp.arange(rows.shape[0], dtype=jnp.int32)
    top = jnp.full((count,), -1e30, jnp.float32)
    scores = (
        lax.dot_general(
            particles, rows, (((1,), (1,)), ((), ())), preferred_element_type=jnp.float32
        )
        * scale
    )
    newtop = jnp.maximum(top, jnp.max(scores, axis=1))
    total = jnp.sum(jnp.exp(scores - newtop[:, None]), axis=1)
    picked = (class_ids[:, None] == (place // orients)[None, :]) & (
        orient_ids[:, None] == (place % orients)[None, :]
    )
    chosen = jnp.sum(jnp.where(picked, scores, 0.0), axis=1)
    top, total, chosen = (newtop, total, chosen)
    gain = (weights * (classes * orients) * jnp.exp(chosen - top) / total).astype(jnp.bfloat16)
    member = class_ids[None, :] == jnp.arange(classes, dtype=jnp.int32)[:, None]
    partial_sums = jnp.zeros((classes, voxels), jnp.float32)
    for step in range(-SHIFT, SHIFT + 1):
        coef = jnp.where(
            member & (offsets[None, :] == step), gain[None, :], jnp.zeros((), jnp.bfloat16)
        )
        moved = jnp.dot(coef, particles, preferred_element_type=jnp.float32)
        moved = jnp.roll(moved.reshape(classes, voxels // NX, NX), step, axis=2).reshape(
            classes, voxels
        )
        partial_sums = partial_sums + moved
    owned = lax.psum_scatter(partial_sums, "cls", scatter_dimension=0, tiled=True)
    owned = lax.psum_scatter(owned, "ptl", scatter_dimension=1, tiled=True)
    population = count * n_cls * n_ptl / classes
    return owned / jnp.sqrt(jnp.float32(population))


def solution(mesh):
    placed = (
        P("cls", "ptl", None),
        P(("cls", "ptl"), None),
        P(("cls", "ptl")),
        P(("cls", "ptl")),
        P(("cls", "ptl")),
        P(("cls", "ptl")),
    )
    planned = mesh.shape["cls"] == 4 and mesh.shape["ptl"] == 8
    return jax.shard_map(
        fused if planned else body,
        mesh=mesh,
        in_specs=placed,
        out_specs=P("cls", "ptl"),
        check_vma=False,
    )
```

```python
import functools
import math

import jax
import jax.numpy as jnp
from jax import lax
from jax.experimental import pallas as pl
from jax.experimental.pallas import tpu as pltpu
from jax.sharding import PartitionSpec as P

NX = 64
SHIFT = 3
MESH = pl.DeviceIdType.MESH

PLAN = (
    (
        (
            (0, 0, 2, 0), (0, 0, 0, 1), (0, 0, 0, 2),
        ),
        (
            (0, 0, 3, 0), (0, 0, 1, 1), (0, 0, 1, 2), (0, 0, 0, 0), (0, 0, 2, 1), (0, 0, 2, 2),
            (0, 1, 0, -1), (2, 0, 0, -1), (1, 0, 2, -1), (2, 0, 0, 0), (1, 0, 2, 1), (0, 0, 3, 2),
            (0, 1, 1, -1), (2, 0, 1, -1), (1, 0, 3, -1), (2, 0, 1, 0), (1, 0, 3, 1), (0, 1, 2, -1),
            (2, 0, 2, -1), (1, 0, 0, -1), (0, 1, 2, 0), (0, 1, 0, 1), (0, 1, 3, -1), (3, 0, 2, -1),
            (3, 0, 0, -1), (3, 0, 2, 2), (0, 1, 3, 0), (0, 1, 1, 1), (3, 0, 0, 2), (0, 2, 0, -1),
            (3, 0, 3, -1), (3, 0, 1, -1), (0, 0, 1, 0), (0, 0, 3, 1), (3, 0, 3, 2), (0, 2, 1, -1),
            (2, 1, 0, -1), (1, 1, 2, -1), (0, 1, 0, 0), (0, 1, 2, 1), (3, 0, 1, 2), (0, 2, 2, -1),
            (2, 1, 1, -1), (1, 1, 3, -1), (0, 1, 1, 0), (0, 1, 3, 1), (0, 2, 3, -1), (2, 0, 3, -1),
            (1, 0, 1, -1),
        ),
        (
            (0, 2, 0, 0), (0, 2, 0, 1), (0, 3, 0, -1), (2, 1, 2, -1), (1, 1, 0, -1), (0, 2, 1, 0),
            (0, 2, 1, 1), (0, 3, 1, -1), (2, 1, 3, -1), (1, 1, 1, -1),
        ),
        (
            (2, 1, 0, 0), (1, 1, 2, 1), (0, 3, 2, -1), (2, 2, 0, -1), (1, 2, 0, -1),
        ),
        (
            (0, 2, 2, 0), (0, 2, 2, 1), (0, 3, 3, -1), (2, 2, 1, -1), (1, 2, 1, -1),
        ),
        (
            (2, 1, 1, 0), (1, 1, 3, 1), (3, 2, 0, -1), (3, 1, 2, -1), (3, 1, 0, -1), (0, 2, 3, 0),
            (0, 2, 3, 1), (3, 3, 2, -1), (2, 2, 2, -1), (1, 2, 2, -1), (0, 3, 0, 0), (0, 3, 0, 1),
            (3, 2, 2, -1), (3, 1, 3, -1), (3, 1, 1, -1), (0, 3, 1, 0), (0, 3, 1, 1), (3, 2, 1, -1),
            (2, 2, 3, -1), (1, 2, 3, -1),
        ),
        (
            (0, 3, 2, 0), (0, 3, 2, 1), (3, 3, 0, -1), (2, 3, 0, -1), (1, 3, 0, -1), (0, 3, 3, 0),
            (0, 3, 3, 1), (3, 2, 3, -1), (2, 3, 1, -1), (1, 3, 1, -1),
        ),
        (
            (3, 3, 3, -1), (2, 3, 2, -1), (1, 3, 2, -1), (3, 3, 1, -1), (2, 3, 3, -1), (1, 3, 3, -1),
        ),
    ),
    (
        (
            (0, 1, 2, 0), (0, 1, 0, 1), (0, 1, 0, 2), (0, 1, 0, 3),
        ),
        (
            (0, 1, 3, 0), (0, 1, 1, 1), (0, 1, 1, 2), (0, 1, 1, 3), (0, 1, 0, 0), (0, 1, 2, 1),
            (0, 1, 2, 2), (0, 1, 2, 3), (0, 0, 0, -1), (0, 2, 0, -1), (2, 1, 0, -1), (1, 1, 2, -1),
            (0, 1, 1, 0), (0, 2, 0, 1), (0, 1, 3, 2), (0, 1, 3, 3), (0, 0, 1, -1), (0, 2, 1, -1),
            (2, 1, 1, -1), (1, 1, 3, -1), (0, 0, 0, 0), (0, 2, 1, 1), (0, 0, 0, 2), (0, 2, 0, 3),
            (0, 0, 2, -1), (0, 2, 2, -1), (2, 1, 2, -1), (1, 1, 0, -1), (0, 2, 2, 0), (0, 1, 3, 1),
            (0, 0, 1, 2), (0, 2, 1, 3), (0, 0, 3, -1), (0, 2, 3, -1), (2, 2, 0, -1), (1, 1, 1, -1),
            (0, 2, 3, 0), (0, 0, 0, 1), (0, 0, 2, 2), (0, 2, 2, 3), (0, 3, 0, -1), (2, 2, 1, -1),
            (1, 0, 0, -1), (2, 2, 0, 0), (1, 1, 2, 1), (0, 0, 3, 2), (0, 2, 3, 3), (0, 3, 1, -1),
            (2, 1, 3, -1), (1, 2, 2, -1), (3, 0, 2, -1), (2, 2, 1, 0), (1, 2, 2, 1), (3, 0, 2, 2),
            (0, 3, 0, 3), (0, 3, 2, -1), (2, 0, 0, -1), (1, 2, 3, -1), (3, 0, 0, -1), (0, 2, 0, 0),
            (1, 2, 3, 1), (3, 0, 0, 2), (0, 3, 1, 3), (0, 3, 3, -1), (3, 1, 2, -1), (3, 2, 0, -1),
            (3, 0, 3, -1),
        ),
        (
            (2, 1, 0, 0), (0, 0, 1, 1), (3, 0, 3, 2), (0, 3, 2, 3), (3, 3, 2, -1), (3, 2, 2, -1),
            (3, 2, 1, -1), (3, 0, 1, -1), (0, 0, 1, 0), (1, 1, 3, 1), (3, 0, 1, 2), (0, 3, 3, 3),
            (3, 3, 0, -1), (3, 2, 3, -1), (1, 2, 0, -1),
        ),
        (
            (0, 2, 1, 0), (0, 0, 2, 1), (3, 2, 0, 3), (3, 3, 3, -1), (2, 0, 1, -1), (3, 1, 0, -1),
        ),
        (
            (2, 1, 1, 0), (0, 2, 2, 1), (3, 3, 2, 3), (3, 3, 1, -1), (3, 1, 3, -1), (1, 0, 1, -1),
        ),
        (
            (0, 0, 2, 0), (0, 0, 3, 1), (3, 2, 2, 3), (2, 0, 2, -1), (1, 2, 1, -1), (0, 0, 3, 0),
            (0, 2, 3, 1), (3, 2, 1, 3), (2, 2, 2, -1), (3, 1, 1, -1), (0, 3, 0, 0), (0, 3, 0, 1),
            (3, 3, 0, 3), (2, 0, 3, -1), (1, 0, 2, -1), (0, 3, 1, 0), (0, 3, 1, 1), (3, 2, 3, 3),
            (2, 2, 3, -1), (1, 0, 3, -1),
        ),
        (
            (0, 3, 2, 0), (0, 3, 2, 1), (3, 3, 3, 3), (2, 3, 0, -1), (1, 3, 0, -1), (0, 3, 3, 0),
            (0, 3, 3, 1), (3, 3, 1, 3), (2, 3, 1, -1), (1, 3, 1, -1),
        ),
        (
            (2, 3, 2, -1), (1, 3, 2, -1), (2, 3, 3, -1), (1, 3, 3, -1),
        ),
    ),
)

GROUPS = (
    (
        ((0, 0), (0, 1), (3, 0), (2, 0)),
        ((1, 0), (0, 2), (2, 1), (1, 1)),
        ((0, 3), (3, 1), (2, 2), (1, 2)),
        ((3, 2), (3, 3), (2, 3), (1, 3)),
    ),
    (
        ((0, 1), (0, 0), (0, 2), (1, 1)),
        ((2, 1), (0, 3), (3, 0), (3, 2)),
        ((3, 3), (1, 2), (3, 1), (2, 0)),
        ((2, 2), (1, 0), (2, 3), (1, 3)),
    ),
)
UNITS = ((), ((0, 0),), ((0, 1),), ((1, 0),), ((1, 1),), ((2, 0),), ((2, 1),), ((3, 0), (3, 1)))
DEPTH = 1024
PARTS = 4
ROWS = 8


def kernel(
    orients, population,
    refs, parts, cid_in, oid_in, off_in, wts_in, out,
    rows, pv, cid, oid, off, wts, top_s, tot_s, cho_s, part, recv1, send2, recv2,
    local_sem, ici_sem, sib_sem, send_sem, r1_sem, r2_sem, s1_sem, s2_sem,
):
    n_cls, n_ptl = part.shape[0], part.shape[1]
    voxels = refs.shape[2]
    half = pv.shape[1]
    cls, ptl = lax.axis_index("cls"), lax.axis_index("ptl")
    core, z = ptl % 2, ptl // 2
    far = z // 2
    sign = 1 - 2 * far
    place = z + far * (3 - 2 * z)
    along_x = cls + 1 - 2 * (cls % 2)
    along_y = cls + 2 - 4 * (cls // 2)
    column = (cls, along_x, along_y, 3 - cls)
    sibling = (cls, ptl + 1 - 2 * core)
    ways = (
        (along_x, ptl),
        (along_y, ptl),
        (cls, ptl + 2 * sign),
        (cls, ptl - 2 * sign),
    )

    def pair(q, zz):
        return column[q] * 4 + zz + far * (3 - 2 * zz)

    barrier = pltpu.get_barrier_semaphore()
    for q in (1, 2, 3):
        pl.semaphore_signal(barrier, inc=1, device_id=(column[q], ptl), device_id_type=MESH)
    for o in range(1, n_ptl):
        pl.semaphore_signal(
            barrier, inc=1, device_id=(cls, lax.rem(ptl + o, n_ptl)), device_id_type=MESH
        )
    loads = [
        pltpu.make_async_copy(parts.at[pl.ds(i * half, half)], pv.at[i], local_sem.at[i])
        for i in range(2)
    ]
    own = cls * 4 + z
    for h in range(2):
        loads.append(
            pltpu.make_async_copy(
                refs.at[0, pl.ds(16 * h, 16)], rows.at[own, core, h], local_sem.at[2 + h]
            )
        )
    for i, (a, b) in enumerate(((cid_in, cid), (oid_in, oid), (off_in, off), (wts_in, wts))):
        loads.append(pltpu.make_async_copy(a, b, local_sem.at[4 + i]))
    for load in loads:
        load.start()
    pl.semaphore_wait(barrier, 3 + n_ptl - 1)

    def chunk(p, c, h):
        return rows.at[p, c, h // 2, :, pl.ds(h % 2 * (voxels // 2), voxels // 2)]

    def own_chunk(h):
        return refs.at[0, pl.ds(16 * (h // 2), 16), pl.ds(h % 2 * (voxels // 2), voxels // 2)]

    def send(src, p, h, way):
        target, recv, idx = (
            (sibling, sib_sem, 4) if way == 4 else (ways[way], ici_sem, way)
        )
        pltpu.make_async_remote_copy(
            src_ref=src,
            dst_ref=chunk(p, core, h),
            send_sem=send_sem.at[idx],
            recv_sem=recv.at[p, h],
            device_id=target,
            device_id_type=MESH,
        ).start()

    def run(section, zc):
        for q, zz, h, way in section:
            p = pair(q, zz)
            block = chunk(p, core, h)
            if way < 0:
                pltpu.make_async_copy(block, block, ici_sem.at[p, h]).wait()
                send(block, p, h, 4)
            elif q == 0 and zz == zc:
                send(own_chunk(h), p, h, way)
            else:
                send(block, p, h, way)

    top_s[...] = jnp.full(top_s.shape, -jnp.inf, jnp.float32)
    tot_s[...] = jnp.zeros(tot_s.shape, jnp.float32)
    cho_s[...] = jnp.zeros(cho_s.shape, jnp.float32)

    def scores(n, group):
        acc = jnp.zeros((len(group) * 64, half), jnp.float32)
        for k in range(0, voxels, DEPTH):
            lhs = jnp.concatenate(
                [rows[p, :, :, :, k : k + DEPTH].reshape(64, DEPTH) for p in group], axis=0
            )
            acc += lax.dot_general(
                lhs,
                pv[n, :, k : k + DEPTH],
                (((1,), (1,)), ((), ())),
                preferred_element_type=jnp.float32,
            )
        sc = acc * (1.0 / math.sqrt(voxels))
        cols = pl.ds(n * half, half)
        old = top_s[:, cols]
        new = jnp.maximum(old, jnp.max(sc, axis=0, keepdims=True))
        top_s[:, cols] = new
        tot_s[:, cols] = tot_s[:, cols] * jnp.exp(old - new) + jnp.sum(
            jnp.exp(sc - new), axis=0, keepdims=True
        )
        wanted = cid[:, cols] * orients + oid[:, cols]
        inner = lax.broadcasted_iota(jnp.int32, (64, half), 0)
        picked = jnp.zeros((1, half), jnp.float32)
        for i, p in enumerate(group):
            mine = inner == wanted - p * 64
            picked += jnp.sum(
                jnp.where(mine, sc[64 * i : 64 * i + 64], 0.0), axis=0, keepdims=True
            )
        cho_s[:, cols] += picked

    groups = [
        [jnp.where(place == 0, pair(*a), pair(*b)) for a, b in zip(first, second)]
        for first, second in zip(*GROUPS)
    ]
    for s, units in enumerate(UNITS):
        for zc in range(2):

            def branch(s=s, zc=zc):
                run(PLAN[zc][s], zc)
                if s == 0:
                    for h in range(PARTS):
                        send(own_chunk(h), own, h, 4)

            pl.when(place == zc)(branch)
        if s == 0:
            for load in loads:
                load.wait()
        for g, n in units:
            if n == 0:
                for p in groups[g]:
                    for h in range(PARTS):
                        block = chunk(p, 1 - core, h)
                        pltpu.make_async_copy(block, block, sib_sem.at[p, h]).wait()
            scores(n, groups[g])

    gain = wts[...] * (n_cls * orients) * jnp.exp(cho_s[...] - top_s[...]) / tot_s[...]
    gain = gain.astype(jnp.bfloat16).astype(jnp.float32)
    code = (off[...] + SHIFT) * ROWS + cid[...]
    steps = 2 * SHIFT + 1
    which = lax.broadcasted_iota(jnp.int32, (steps * ROWS, 2 * half), 0)
    coef = jnp.where(which == code, gain, 0.0).astype(jnp.bfloat16)
    width = voxels // n_ptl
    lane = lax.broadcasted_iota(jnp.int32, (ROWS, 128), 1) % NX
    for j in range(n_ptl):
        pixels = pv[:, :, j * width : (j + 1) * width].reshape(2 * half, width)
        moved = jnp.dot(coef, pixels, preferred_element_type=jnp.float32)
        for v in range(width // 128):
            total = jnp.zeros((ROWS, 128), jnp.float32)
            for i, step in enumerate(range(-SHIFT, SHIFT + 1)):
                a = moved[i * ROWS : (i + 1) * ROWS, v * 128 : (v + 1) * 128]
                if step == 0:
                    total += a
                    continue
                inside = pltpu.roll(a, step % 128, 1)
                across = pltpu.roll(a, (step + NX) % 128, 1)
                keep = lane >= step if step > 0 else lane < NX + step
                total += jnp.where(keep, inside, across)
            for c in range(n_cls):
                part[c, j : j + 1, v * 128 : (v + 1) * 128] = total[c : c + 1]

    copies = []
    for q in (1, 2, 3):
        copies.append(
            pltpu.make_async_remote_copy(
                src_ref=part.at[column[q]],
                dst_ref=recv1.at[q - 1],
                send_sem=s1_sem.at[q - 1],
                recv_sem=r1_sem.at[q - 1],
                device_id=(column[q], ptl),
                device_id_type=MESH,
            )
        )
        copies[-1].start()
    for copy in copies:
        copy.wait_recv()
    mine = part[cls] + recv1[0] + recv1[1] + recv1[2]
    for j in range(n_ptl):
        send2[j] = mine[j : j + 1]
    for o in range(1, n_ptl):
        to = lax.rem(ptl + o, n_ptl)
        copies.append(
            pltpu.make_async_remote_copy(
                src_ref=send2.at[to],
                dst_ref=recv2.at[o - 1],
                send_sem=s2_sem.at[o - 1],
                recv_sem=r2_sem.at[o - 1],
                device_id=(cls, to),
                device_id_type=MESH,
            )
        )
        copies[-1].start()
    total = send2[ptl]
    for o in range(1, n_ptl):
        copies[2 + o].wait_recv()
        total += recv2[o - 1]
    out[...] = total / jnp.sqrt(jnp.float32(population))
    for copy in copies:
        copy.wait_send()

    def sent(count, idx):
        gone = rows.at[pl.ds(0, count), 0]
        pltpu.make_async_copy(gone, gone, send_sem.at[idx]).wait()

    sent(5, 0)
    sent(5, 1)
    sent(16, 4)

    @pl.when(place == 0)
    def _():
        sent(2, 2)

    @pl.when(place == 1)
    def _():
        sent(3, 2)
        sent(5, 3)


def fused(references, particles, class_ids, orient_ids, offsets, weights):
    n_cls = lax.axis_size("cls")
    n_ptl = lax.axis_size("ptl")
    _, local_ori, voxels = references.shape
    count = particles.shape[0]
    orients = local_ori * n_ptl
    population = count * n_ptl
    line = [x.reshape(1, count) for x in (class_ids, orient_ids, offsets, weights)]
    f32 = jnp.float32
    vmem = pl.BlockSpec(memory_space=pltpu.VMEM)
    hbm = pl.BlockSpec(memory_space=pl.ANY)
    return pl.pallas_call(
        functools.partial(kernel, orients, population),
        out_shape=jax.ShapeDtypeStruct((1, voxels // n_ptl), f32),
        in_specs=[hbm] * 6,
        out_specs=vmem,
        scratch_shapes=[
            pltpu.VMEM((n_cls * n_ptl // 2, 2, 2, local_ori // 2, voxels), references.dtype),
            pltpu.VMEM((2, count // 2, voxels), particles.dtype),
            *[pltpu.VMEM((1, count), x.dtype) for x in line],
            pltpu.VMEM((1, count), f32),
            pltpu.VMEM((1, count), f32),
            pltpu.VMEM((1, count), f32),
            pltpu.VMEM((n_cls, n_ptl, voxels // n_ptl), f32),
            pltpu.VMEM((n_cls - 1, n_ptl, voxels // n_ptl), f32),
            pltpu.VMEM((n_ptl, 1, voxels // n_ptl), f32),
            pltpu.VMEM((n_ptl - 1, 1, voxels // n_ptl), f32),
            pltpu.SemaphoreType.DMA((8,)),
            pltpu.SemaphoreType.DMA((n_cls * n_ptl // 2, PARTS)),
            pltpu.SemaphoreType.DMA((n_cls * n_ptl // 2, PARTS)),
            pltpu.SemaphoreType.DMA((5,)),
            pltpu.SemaphoreType.DMA((n_cls - 1,)),
            pltpu.SemaphoreType.DMA((n_ptl - 1,)),
            pltpu.SemaphoreType.DMA((n_cls - 1,)),
            pltpu.SemaphoreType.DMA((n_ptl - 1,)),
        ],
        compiler_params=pltpu.CompilerParams(
            collective_id=0, has_side_effects=True, vmem_limit_bytes=60 * 1024 * 1024
        ),
        cost_estimate=pl.CostEstimate(
            flops=2 * count * voxels * n_cls * orients,
            bytes_accessed=2 * voxels * (count + n_cls * orients),
            transcendentals=count * n_cls * orients,
        ),
    )(references, particles, *line)


def body(references, particles, class_ids, orient_ids, offsets, weights):
    n_cls = lax.axis_size("cls")
    n_ptl = lax.axis_size("ptl")
    per_owner, local_ori, voxels = references.shape
    orients = local_ori * n_ptl
    classes = per_owner * n_cls
    count = particles.shape[0]
    scale = 1.0 / math.sqrt(voxels)
    class_block = lax.all_gather(references, "ptl", axis=1, tiled=True)
    piece = lax.all_gather(class_block, "cls", axis=0, tiled=True)
    rows = piece.reshape(piece.shape[0] * orients, voxels)
    place = jnp.arange(rows.shape[0], dtype=jnp.int32)
    top = jnp.full((count,), -1e30, jnp.float32)
    scores = (
        lax.dot_general(
            particles, rows, (((1,), (1,)), ((), ())), preferred_element_type=jnp.float32
        )
        * scale
    )
    newtop = jnp.maximum(top, jnp.max(scores, axis=1))
    total = jnp.sum(jnp.exp(scores - newtop[:, None]), axis=1)
    picked = (class_ids[:, None] == (place // orients)[None, :]) & (
        orient_ids[:, None] == (place % orients)[None, :]
    )
    chosen = jnp.sum(jnp.where(picked, scores, 0.0), axis=1)
    top, total, chosen = (newtop, total, chosen)
    gain = (weights * (classes * orients) * jnp.exp(chosen - top) / total).astype(jnp.bfloat16)
    member = class_ids[None, :] == jnp.arange(classes, dtype=jnp.int32)[:, None]
    partial_sums = jnp.zeros((classes, voxels), jnp.float32)
    for step in range(-SHIFT, SHIFT + 1):
        coef = jnp.where(
            member & (offsets[None, :] == step), gain[None, :], jnp.zeros((), jnp.bfloat16)
        )
        moved = jnp.dot(coef, particles, preferred_element_type=jnp.float32)
        moved = jnp.roll(moved.reshape(classes, voxels // NX, NX), step, axis=2).reshape(
            classes, voxels
        )
        partial_sums = partial_sums + moved
    owned = lax.psum_scatter(partial_sums, "cls", scatter_dimension=0, tiled=True)
    owned = lax.psum_scatter(owned, "ptl", scatter_dimension=1, tiled=True)
    population = count * n_cls * n_ptl / classes
    return owned / jnp.sqrt(jnp.float32(population))


def solution(mesh):
    placed = (
        P("cls", "ptl", None),
        P(("cls", "ptl"), None),
        P(("cls", "ptl")),
        P(("cls", "ptl")),
        P(("cls", "ptl")),
        P(("cls", "ptl")),
    )
    planned = mesh.shape["cls"] == 4 and mesh.shape["ptl"] == 8
    return jax.shard_map(
        fused if planned else body,
        mesh=mesh,
        in_specs=placed,
        out_specs=P("cls", "ptl"),
        check_vma=False,
    )
```

```python
import functools
import math

import jax
import jax.numpy as jnp
from jax import lax
from jax.experimental import pallas as pl
from jax.experimental.pallas import tpu as pltpu
from jax.sharding import PartitionSpec as P

NX = 64
SHIFT = 3
MESH = pl.DeviceIdType.MESH

PLAN = (
    (
        (
            (0, 0, 1, 0), (0, 0, 0, 1), (0, 0, 0, 2), (0, 0, 0, 0), (0, 0, 1, 1), (0, 0, 1, 2),
        ),
        (
            (0, 1, 0, -1), (2, 0, 0, -1), (1, 0, 1, -1), (2, 0, 0, 0), (1, 0, 1, 1), (0, 1, 0, 1),
            (0, 1, 1, -1), (2, 0, 1, -1), (1, 0, 0, -1), (0, 1, 1, 0), (0, 1, 0, 4), (2, 0, 0, 4),
            (1, 0, 0, 4),
        ),
        (
            (0, 1, 0, 0), (0, 1, 1, 1),
        ),
        (
            (0, 2, 0, -1), (3, 0, 1, -1), (3, 0, 0, -1), (3, 0, 1, 2), (3, 0, 0, 2), (3, 0, 0, 4),
            (0, 2, 0, 0), (0, 2, 0, 1), (0, 2, 1, -1), (2, 1, 0, -1), (1, 1, 1, -1), (0, 2, 0, 4),
            (0, 2, 1, 0), (0, 2, 1, 1), (0, 3, 0, -1), (2, 1, 1, -1), (1, 1, 0, -1), (2, 1, 0, 4),
            (1, 1, 0, 4), (2, 1, 0, 0), (1, 1, 1, 1), (0, 3, 1, -1), (2, 2, 0, -1), (1, 2, 0, -1),
            (0, 3, 0, 4),
        ),
        (
            (0, 3, 0, 0), (0, 3, 0, 1),
        ),
        (
            (3, 2, 0, -1), (2, 2, 1, -1), (1, 2, 1, -1), (2, 2, 0, 4), (1, 2, 0, 4), (0, 3, 1, 0),
            (0, 3, 1, 1), (3, 2, 1, -1), (3, 1, 1, -1), (3, 1, 0, -1), (3, 2, 0, 4), (3, 1, 0, 4),
        ),
        (
        ),
        (
            (3, 3, 1, -1), (2, 3, 0, -1), (1, 3, 0, -1), (3, 3, 0, -1), (2, 3, 1, -1), (1, 3, 1, -1),
            (3, 3, 0, 4), (2, 3, 0, 4), (1, 3, 0, 4),
        ),
    ),
    (
        (
            (0, 1, 1, 0), (0, 1, 0, 1), (0, 1, 0, 2), (0, 1, 0, 3), (0, 1, 0, 0), (0, 1, 1, 1),
            (0, 1, 1, 2), (0, 1, 1, 3),
        ),
        (
            (0, 0, 0, -1), (0, 2, 0, -1), (2, 1, 0, -1), (1, 1, 1, -1), (0, 0, 0, 0), (0, 2, 0, 1),
            (0, 0, 0, 2), (0, 2, 0, 3), (0, 0, 0, 1), (0, 0, 1, -1), (0, 2, 1, -1), (2, 1, 1, -1),
            (1, 1, 0, -1), (0, 2, 1, 0), (0, 0, 1, 2), (0, 2, 1, 3), (0, 0, 0, 4), (0, 2, 0, 4),
            (2, 1, 0, 4), (1, 1, 0, 4),
        ),
        (
            (1, 1, 1, 1),
        ),
        (
            (0, 3, 0, -1), (2, 2, 0, -1), (1, 0, 0, -1), (2, 2, 0, 0), (0, 3, 0, 3), (0, 2, 0, 0),
            (0, 3, 1, -1), (2, 0, 0, -1), (1, 2, 1, -1), (1, 2, 1, 1), (0, 3, 1, 3), (0, 3, 0, 4),
            (2, 1, 0, 0), (0, 0, 1, 1), (3, 0, 1, -1), (3, 0, 1, 2), (3, 1, 1, -1), (3, 2, 0, -1),
            (3, 2, 0, 3), (0, 0, 1, 0), (0, 2, 1, 1), (3, 0, 0, -1), (3, 0, 0, 2), (3, 0, 0, 4),
            (3, 2, 1, -1), (1, 2, 0, -1), (3, 2, 1, 3), (1, 2, 0, 4), (3, 2, 0, 4),
        ),
        (
            (0, 3, 0, 0), (0, 3, 0, 1), (3, 3, 1, -1), (3, 3, 1, 3),
        ),
        (
            (2, 0, 1, -1), (3, 1, 0, -1), (2, 0, 0, 4), (3, 1, 0, 4), (0, 3, 1, 0), (0, 3, 1, 1),
            (3, 3, 0, -1), (3, 3, 0, 3), (3, 3, 0, 4), (2, 2, 1, -1), (1, 0, 1, -1), (2, 2, 0, 4),
            (1, 0, 0, 4),
        ),
        (
        ),
        (
            (2, 3, 0, -1), (1, 3, 0, -1), (2, 3, 1, -1), (1, 3, 1, -1), (2, 3, 0, 4), (1, 3, 0, 4),
        ),
    ),
)

GROUPS = (
    (
        ((0, 0), (0, 1), (2, 0), (1, 0)),
        ((3, 0), (0, 2), (2, 1), (1, 1)),
        ((0, 3), (2, 2), (1, 2), (3, 2)),
        ((3, 1), (3, 3), (2, 3), (1, 3)),
    ),
    (
        ((0, 1), (0, 0), (0, 2), (2, 1)),
        ((1, 1), (0, 3), (3, 0), (1, 2)),
        ((3, 2), (2, 0), (3, 1), (3, 3)),
        ((2, 2), (1, 0), (2, 3), (1, 3)),
    ),
)
UNITS = ((), ((0, 0),), ((0, 1),), ((1, 0),), ((1, 1),), ((2, 0),), ((2, 1),), ((3, 0), (3, 1)))
DEPTH = 1024
ROWS = 8


def kernel(
    orients, population,
    refs, parts, cid_in, oid_in, off_in, wts_in, out,
    rows, pv, cid, oid, off, wts, top_s, tot_s, cho_s, part, recv1, send2, recv2,
    local_sem, ici_sem, sib_sem, send_sem, r1_sem, r2_sem, s1_sem, s2_sem,
):
    n_cls, n_ptl = part.shape[0], part.shape[1]
    voxels = refs.shape[2]
    half = pv.shape[1]
    cls, ptl = lax.axis_index("cls"), lax.axis_index("ptl")
    core, z = ptl % 2, ptl // 2
    far = z // 2
    sign = 1 - 2 * far
    place = z + far * (3 - 2 * z)
    along_x = cls + 1 - 2 * (cls % 2)
    along_y = cls + 2 - 4 * (cls // 2)
    column = (cls, along_x, along_y, 3 - cls)
    ways = (
        (along_x, ptl),
        (along_y, ptl),
        (cls, ptl + 2 * sign),
        (cls, ptl - 2 * sign),
        (cls, ptl + 1 - 2 * core),
    )

    def pair(q, zz):
        return column[q] * 4 + zz + far * (3 - 2 * zz)

    barrier = pltpu.get_barrier_semaphore()
    for q in (1, 2, 3):
        pl.semaphore_signal(barrier, inc=1, device_id=(column[q], ptl), device_id_type=MESH)
    for o in range(1, n_ptl):
        pl.semaphore_signal(
            barrier, inc=1, device_id=(cls, lax.rem(ptl + o, n_ptl)), device_id_type=MESH
        )
    loads = [
        pltpu.make_async_copy(parts.at[pl.ds(i * half, half)], pv.at[i], local_sem.at[i])
        for i in range(2)
    ]
    own = cls * 4 + z
    loads.append(pltpu.make_async_copy(refs.at[0], rows.at[own, core], local_sem.at[2]))
    for i, (a, b) in enumerate(((cid_in, cid), (oid_in, oid), (off_in, off), (wts_in, wts))):
        loads.append(pltpu.make_async_copy(a, b, local_sem.at[3 + i]))
    for load in loads:
        load.start()
    pl.semaphore_wait(barrier, 3 + n_ptl - 1)

    def chunk(p, h):
        return rows.at[p, core, pl.ds(16 * h, 16)]

    def send(src, p, h, way):
        pltpu.make_async_remote_copy(
            src_ref=src,
            dst_ref=chunk(p, h) if way < 4 else rows.at[p, core],
            send_sem=send_sem.at[way],
            recv_sem=ici_sem.at[p, h] if way < 4 else sib_sem.at[p],
            device_id=ways[way],
            device_id_type=MESH,
        ).start()

    def run(section, zc):
        for q, zz, h, way in section:
            p = pair(q, zz)
            block = chunk(p, h)
            if way < 0:
                pltpu.make_async_copy(block, block, ici_sem.at[p, h]).wait()
            elif way == 4:
                send(rows.at[p, core], p, h, way)
            elif q == 0 and zz == zc:
                send(refs.at[0, pl.ds(16 * h, 16)], p, h, way)
            else:
                send(block, p, h, way)

    top_s[...] = jnp.full(top_s.shape, -jnp.inf, jnp.float32)
    tot_s[...] = jnp.zeros(tot_s.shape, jnp.float32)
    cho_s[...] = jnp.zeros(cho_s.shape, jnp.float32)

    def scores(n, group):
        acc = jnp.zeros((len(group) * 64, half), jnp.float32)
        for k in range(0, voxels, DEPTH):
            lhs = jnp.concatenate(
                [rows[p, :, :, k : k + DEPTH].reshape(64, DEPTH) for p in group], axis=0
            )
            acc += lax.dot_general(
                lhs,
                pv[n, :, k : k + DEPTH],
                (((1,), (1,)), ((), ())),
                preferred_element_type=jnp.float32,
            )
        sc = acc * (1.0 / math.sqrt(voxels))
        cols = pl.ds(n * half, half)
        old = top_s[:, cols]
        new = jnp.maximum(old, jnp.max(sc, axis=0, keepdims=True))
        top_s[:, cols] = new
        tot_s[:, cols] = tot_s[:, cols] * jnp.exp(old - new) + jnp.sum(
            jnp.exp(sc - new), axis=0, keepdims=True
        )
        wanted = cid[:, cols] * orients + oid[:, cols]
        inner = lax.broadcasted_iota(jnp.int32, (64, half), 0)
        picked = jnp.zeros((1, half), jnp.float32)
        for i, p in enumerate(group):
            mine = inner == wanted - p * 64
            picked += jnp.sum(
                jnp.where(mine, sc[64 * i : 64 * i + 64], 0.0), axis=0, keepdims=True
            )
        cho_s[:, cols] += picked

    groups = [
        [jnp.where(place == 0, pair(*a), pair(*b)) for a, b in zip(first, second)]
        for first, second in zip(*GROUPS)
    ]
    for s, units in enumerate(UNITS):
        for zc in range(2):

            def branch(s=s, zc=zc):
                run(PLAN[zc][s], zc)
                if s == 0:
                    send(refs.at[0], own, 0, 4)

            pl.when(place == zc)(branch)
        if s == 0:
            for load in loads:
                load.wait()
        for g, n in units:
            if n == 0:
                for p in groups[g]:
                    block = rows.at[p, 1 - core]
                    pltpu.make_async_copy(block, block, sib_sem.at[p]).wait()
            scores(n, groups[g])

    gain = wts[...] * (n_cls * orients) * jnp.exp(cho_s[...] - top_s[...]) / tot_s[...]
    gain = gain.astype(jnp.bfloat16).astype(jnp.float32)
    code = (off[...] + SHIFT) * ROWS + cid[...]
    steps = 2 * SHIFT + 1
    which = lax.broadcasted_iota(jnp.int32, (steps * ROWS, 2 * half), 0)
    coef = jnp.where(which == code, gain, 0.0).astype(jnp.bfloat16)
    width = voxels // n_ptl
    lane = lax.broadcasted_iota(jnp.int32, (ROWS, 128), 1) % NX
    for j in range(n_ptl):
        pixels = pv[:, :, j * width : (j + 1) * width].reshape(2 * half, width)
        moved = jnp.dot(coef, pixels, preferred_element_type=jnp.float32)
        for v in range(width // 128):
            total = jnp.zeros((ROWS, 128), jnp.float32)
            for i, step in enumerate(range(-SHIFT, SHIFT + 1)):
                a = moved[i * ROWS : (i + 1) * ROWS, v * 128 : (v + 1) * 128]
                if step == 0:
                    total += a
                    continue
                inside = pltpu.roll(a, step % 128, 1)
                across = pltpu.roll(a, (step + NX) % 128, 1)
                keep = lane >= step if step > 0 else lane < NX + step
                total += jnp.where(keep, inside, across)
            for c in range(n_cls):
                part[c, j : j + 1, v * 128 : (v + 1) * 128] = total[c : c + 1]

    copies = []
    for q in (1, 2, 3):
        copies.append(
            pltpu.make_async_remote_copy(
                src_ref=part.at[column[q]],
                dst_ref=recv1.at[q - 1],
                send_sem=s1_sem.at[q - 1],
                recv_sem=r1_sem.at[q - 1],
                device_id=(column[q], ptl),
                device_id_type=MESH,
            )
        )
        copies[-1].start()
    for copy in copies:
        copy.wait_recv()
    mine = part[cls] + recv1[0] + recv1[1] + recv1[2]
    for j in range(n_ptl):
        send2[j] = mine[j : j + 1]
    for o in range(1, n_ptl):
        to = lax.rem(ptl + o, n_ptl)
        copies.append(
            pltpu.make_async_remote_copy(
                src_ref=send2.at[to],
                dst_ref=recv2.at[o - 1],
                send_sem=s2_sem.at[o - 1],
                recv_sem=r2_sem.at[o - 1],
                device_id=(cls, to),
                device_id_type=MESH,
            )
        )
        copies[-1].start()
    total = send2[ptl]
    for o in range(1, n_ptl):
        copies[2 + o].wait_recv()
        total += recv2[o - 1]
    out[...] = total / jnp.sqrt(jnp.float32(population))
    for copy in copies:
        copy.wait_send()

    def sent(count, idx):
        gone = rows.at[pl.ds(0, count), 0]
        pltpu.make_async_copy(gone, gone, send_sem.at[idx]).wait()

    sent(5, 0)
    sent(5, 1)
    sent(16, 4)

    @pl.when(place == 0)
    def _():
        sent(2, 2)

    @pl.when(place == 1)
    def _():
        sent(3, 2)
        sent(5, 3)


def fused(references, particles, class_ids, orient_ids, offsets, weights):
    n_cls = lax.axis_size("cls")
    n_ptl = lax.axis_size("ptl")
    _, local_ori, voxels = references.shape
    count = particles.shape[0]
    orients = local_ori * n_ptl
    population = count * n_ptl
    line = [x.reshape(1, count) for x in (class_ids, orient_ids, offsets, weights)]
    f32 = jnp.float32
    vmem = pl.BlockSpec(memory_space=pltpu.VMEM)
    hbm = pl.BlockSpec(memory_space=pl.ANY)
    return pl.pallas_call(
        functools.partial(kernel, orients, population),
        out_shape=jax.ShapeDtypeStruct((1, voxels // n_ptl), f32),
        in_specs=[hbm] * 6,
        out_specs=vmem,
        scratch_shapes=[
            pltpu.VMEM((n_cls * n_ptl // 2, 2, local_ori, voxels), references.dtype),
            pltpu.VMEM((2, count // 2, voxels), particles.dtype),
            *[pltpu.VMEM((1, count), x.dtype) for x in line],
            pltpu.VMEM((1, count), f32),
            pltpu.VMEM((1, count), f32),
            pltpu.VMEM((1, count), f32),
            pltpu.VMEM((n_cls, n_ptl, voxels // n_ptl), f32),
            pltpu.VMEM((n_cls - 1, n_ptl, voxels // n_ptl), f32),
            pltpu.VMEM((n_ptl, 1, voxels // n_ptl), f32),
            pltpu.VMEM((n_ptl - 1, 1, voxels // n_ptl), f32),
            pltpu.SemaphoreType.DMA((7,)),
            pltpu.SemaphoreType.DMA((n_cls * n_ptl // 2, 2)),
            pltpu.SemaphoreType.DMA((n_cls * n_ptl // 2,)),
            pltpu.SemaphoreType.DMA((5,)),
            pltpu.SemaphoreType.DMA((n_cls - 1,)),
            pltpu.SemaphoreType.DMA((n_ptl - 1,)),
            pltpu.SemaphoreType.DMA((n_cls - 1,)),
            pltpu.SemaphoreType.DMA((n_ptl - 1,)),
        ],
        compiler_params=pltpu.CompilerParams(
            collective_id=0, has_side_effects=True, vmem_limit_bytes=60 * 1024 * 1024
        ),
        cost_estimate=pl.CostEstimate(
            flops=2 * count * voxels * n_cls * orients,
            bytes_accessed=2 * voxels * (count + n_cls * orients),
            transcendentals=count * n_cls * orients,
        ),
    )(references, particles, *line)


def body(references, particles, class_ids, orient_ids, offsets, weights):
    n_cls = lax.axis_size("cls")
    n_ptl = lax.axis_size("ptl")
    per_owner, local_ori, voxels = references.shape
    orients = local_ori * n_ptl
    classes = per_owner * n_cls
    count = particles.shape[0]
    scale = 1.0 / math.sqrt(voxels)
    class_block = lax.all_gather(references, "ptl", axis=1, tiled=True)
    piece = lax.all_gather(class_block, "cls", axis=0, tiled=True)
    rows = piece.reshape(piece.shape[0] * orients, voxels)
    place = jnp.arange(rows.shape[0], dtype=jnp.int32)
    top = jnp.full((count,), -1e30, jnp.float32)
    scores = (
        lax.dot_general(
            particles, rows, (((1,), (1,)), ((), ())), preferred_element_type=jnp.float32
        )
        * scale
    )
    newtop = jnp.maximum(top, jnp.max(scores, axis=1))
    total = jnp.sum(jnp.exp(scores - newtop[:, None]), axis=1)
    picked = (class_ids[:, None] == (place // orients)[None, :]) & (
        orient_ids[:, None] == (place % orients)[None, :]
    )
    chosen = jnp.sum(jnp.where(picked, scores, 0.0), axis=1)
    top, total, chosen = (newtop, total, chosen)
    gain = (weights * (classes * orients) * jnp.exp(chosen - top) / total).astype(jnp.bfloat16)
    member = class_ids[None, :] == jnp.arange(classes, dtype=jnp.int32)[:, None]
    partial_sums = jnp.zeros((classes, voxels), jnp.float32)
    for step in range(-SHIFT, SHIFT + 1):
        coef = jnp.where(
            member & (offsets[None, :] == step), gain[None, :], jnp.zeros((), jnp.bfloat16)
        )
        moved = jnp.dot(coef, particles, preferred_element_type=jnp.float32)
        moved = jnp.roll(moved.reshape(classes, voxels // NX, NX), step, axis=2).reshape(
            classes, voxels
        )
        partial_sums = partial_sums + moved
    owned = lax.psum_scatter(partial_sums, "cls", scatter_dimension=0, tiled=True)
    owned = lax.psum_scatter(owned, "ptl", scatter_dimension=1, tiled=True)
    population = count * n_cls * n_ptl / classes
    return owned / jnp.sqrt(jnp.float32(population))


def solution(mesh):
    placed = (
        P("cls", "ptl", None),
        P(("cls", "ptl"), None),
        P(("cls", "ptl")),
        P(("cls", "ptl")),
        P(("cls", "ptl")),
        P(("cls", "ptl")),
    )
    planned = mesh.shape["cls"] == 4 and mesh.shape["ptl"] == 8
    return jax.shard_map(
        fused if planned else body,
        mesh=mesh,
        in_specs=placed,
        out_specs=P("cls", "ptl"),
        check_vma=False,
    )
```

```python
import functools
import math

import jax
import jax.numpy as jnp
from jax import lax
from jax.experimental import pallas as pl
from jax.experimental.pallas import tpu as pltpu
from jax.sharding import PartitionSpec as P

NX = 64
SHIFT = 3
MESH = pl.DeviceIdType.MESH

PLAN = (
    (
        (
            (0, 0, 1, 0), (0, 0, 0, 1), (0, 0, 0, 2), (0, 0, 0, 0), (0, 0, 1, 1), (0, 0, 1, 2),
        ),
        (
            (0, 1, 0, -1), (2, 0, 0, -1), (1, 0, 1, -1), (2, 0, 0, 0), (1, 0, 1, 1), (0, 1, 0, 1),
        ),
        (
            (0, 1, 0, 0), (0, 1, 1, -1), (2, 0, 1, -1), (1, 0, 0, -1), (0, 1, 1, 0), (0, 1, 1, 1),
        ),
        (
            (0, 2, 0, -1), (3, 0, 1, -1), (3, 0, 0, -1), (3, 0, 1, 2), (3, 0, 0, 2), (0, 2, 0, 0),
            (0, 2, 0, 1),
        ),
        (
            (0, 2, 1, -1), (2, 1, 0, -1), (1, 1, 1, -1), (0, 2, 1, 0), (0, 2, 1, 1),
        ),
        (
            (2, 1, 0, 0), (1, 1, 1, 1), (0, 3, 0, -1), (2, 1, 1, -1), (1, 1, 0, -1),
        ),
        (
            (0, 3, 0, 0), (0, 3, 0, 1), (0, 3, 1, -1), (2, 2, 0, -1), (1, 2, 0, -1),
        ),
        (
            (0, 3, 1, 0), (0, 3, 1, 1), (3, 2, 0, -1), (2, 2, 1, -1), (1, 2, 1, -1),
        ),
        (
            (3, 3, 1, -1), (3, 1, 1, -1), (3, 1, 0, -1),
        ),
        (
            (3, 2, 1, -1), (2, 3, 0, -1), (1, 3, 0, -1),
        ),
        (
            (3, 3, 0, -1), (2, 3, 1, -1), (1, 3, 1, -1),
        ),
    ),
    (
        (
            (0, 1, 1, 0), (0, 1, 0, 1), (0, 1, 0, 2), (0, 1, 0, 3), (0, 1, 0, 0), (0, 1, 1, 1),
            (0, 1, 1, 2), (0, 1, 1, 3),
        ),
        (
            (0, 0, 0, -1), (0, 2, 0, -1), (2, 1, 0, -1), (1, 1, 1, -1), (0, 0, 0, 0), (0, 2, 0, 1),
            (0, 0, 0, 2), (0, 2, 0, 3), (0, 0, 0, 1),
        ),
        (
            (1, 1, 1, 1), (0, 0, 1, -1), (0, 2, 1, -1), (2, 1, 1, -1), (1, 1, 0, -1), (0, 2, 1, 0),
            (0, 0, 1, 2), (0, 2, 1, 3),
        ),
        (
            (0, 2, 0, 0), (0, 3, 0, -1), (2, 2, 0, -1), (1, 0, 0, -1), (2, 2, 0, 0), (0, 3, 0, 3),
        ),
        (
            (2, 1, 0, 0), (0, 0, 1, 1), (0, 3, 1, -1), (2, 0, 0, -1), (1, 2, 1, -1), (1, 2, 1, 1),
            (0, 3, 1, 3), (3, 0, 1, -1), (3, 0, 1, 2),
        ),
        (
            (0, 0, 1, 0), (0, 2, 1, 1), (3, 1, 1, -1), (3, 2, 0, -1), (3, 2, 0, 3), (3, 0, 0, -1),
            (3, 0, 0, 2), (3, 3, 1, -1), (3, 3, 1, 3),
        ),
        (
            (0, 3, 0, 0), (0, 3, 0, 1), (3, 2, 1, -1), (1, 2, 0, -1), (3, 2, 1, 3), (3, 3, 0, -1),
        ),
        (
            (0, 3, 1, 0), (0, 3, 1, 1), (3, 3, 0, 3), (2, 0, 1, -1), (3, 1, 0, -1),
        ),
        (
            (2, 2, 1, -1), (1, 0, 1, -1),
        ),
        (
            (2, 3, 0, -1), (1, 3, 0, -1),
        ),
        (
            (2, 3, 1, -1), (1, 3, 1, -1),
        ),
    ),
)

GROUPS = (
    (
        ((0, 0), (0, 1), (2, 0), (1, 0)),
        ((3, 0), (0, 2), (2, 1), (1, 1)),
        ((0, 3), (2, 2), (1, 2), (3, 1)),
        ((3, 2), (3, 3), (2, 3), (1, 3)),
    ),
    (
        ((0, 1), (0, 0), (0, 2), (2, 1)),
        ((1, 1), (0, 3), (3, 0), (1, 2)),
        ((3, 2), (3, 3), (2, 0), (3, 1)),
        ((2, 2), (1, 0), (2, 3), (1, 3)),
    ),
)
UNITS = ((), (), ((0, 0),), ((0, 1),), (), (), ((1, 0),), ((1, 1),), ((2, 0),), ((2, 1),), ((3, 0), (3, 1)))
DEPTH = 1024
ROWS = 8


def kernel(
    orients, population,
    refs, parts, cid_in, oid_in, off_in, wts_in, out,
    rows, pv, cid, oid, off, wts, top_s, tot_s, cho_s, part, recv1, send2, recv2,
    local_sem, ici_sem, sib_sem, send_sem, r1_sem, r2_sem, s1_sem, s2_sem,
):
    n_cls, n_ptl = part.shape[0], part.shape[1]
    voxels = refs.shape[2]
    half = pv.shape[1]
    cls, ptl = lax.axis_index("cls"), lax.axis_index("ptl")
    core, z = ptl % 2, ptl // 2
    far = z // 2
    sign = 1 - 2 * far
    place = z + far * (3 - 2 * z)
    along_x = cls + 1 - 2 * (cls % 2)
    along_y = cls + 2 - 4 * (cls // 2)
    column = (cls, along_x, along_y, 3 - cls)
    sibling = (cls, ptl + 1 - 2 * core)
    ways = (
        (along_x, ptl),
        (along_y, ptl),
        (cls, ptl + 2 * sign),
        (cls, ptl - 2 * sign),
    )

    def pair(q, zz):
        return column[q] * 4 + zz + far * (3 - 2 * zz)

    barrier = pltpu.get_barrier_semaphore()
    for q in (1, 2, 3):
        pl.semaphore_signal(barrier, inc=1, device_id=(column[q], ptl), device_id_type=MESH)
    for o in range(1, n_ptl):
        pl.semaphore_signal(
            barrier, inc=1, device_id=(cls, lax.rem(ptl + o, n_ptl)), device_id_type=MESH
        )
    loads = [
        pltpu.make_async_copy(parts.at[pl.ds(i * half, half)], pv.at[i], local_sem.at[i])
        for i in range(2)
    ]
    own = cls * 4 + z
    for h in range(2):
        loads.append(
            pltpu.make_async_copy(
                refs.at[0, pl.ds(16 * h, 16)], rows.at[own, core, h], local_sem.at[2 + h]
            )
        )
    for i, (a, b) in enumerate(((cid_in, cid), (oid_in, oid), (off_in, off), (wts_in, wts))):
        loads.append(pltpu.make_async_copy(a, b, local_sem.at[4 + i]))
    for load in loads:
        load.start()
    pl.semaphore_wait(barrier, 3 + n_ptl - 1)

    def send(src, p, h, way):
        target, recv, idx = (
            (sibling, sib_sem, 4) if way == 4 else (ways[way], ici_sem, way)
        )
        pltpu.make_async_remote_copy(
            src_ref=src,
            dst_ref=rows.at[p, core, h],
            send_sem=send_sem.at[idx],
            recv_sem=recv.at[p, h],
            device_id=target,
            device_id_type=MESH,
        ).start()

    def run(section, zc):
        for q, zz, h, way in section:
            p = pair(q, zz)
            block = rows.at[p, core, h]
            if way < 0:
                pltpu.make_async_copy(block, block, ici_sem.at[p, h]).wait()
                send(block, p, h, 4)
            elif q == 0 and zz == zc:
                send(refs.at[0, pl.ds(16 * h, 16)], p, h, way)
            else:
                send(block, p, h, way)

    top_s[...] = jnp.full(top_s.shape, -jnp.inf, jnp.float32)
    tot_s[...] = jnp.zeros(tot_s.shape, jnp.float32)
    cho_s[...] = jnp.zeros(cho_s.shape, jnp.float32)

    def scores(n, group):
        acc = jnp.zeros((len(group) * 64, half), jnp.float32)
        for k in range(0, voxels, DEPTH):
            lhs = jnp.concatenate(
                [rows[p, :, :, :, k : k + DEPTH].reshape(64, DEPTH) for p in group], axis=0
            )
            acc += lax.dot_general(
                lhs,
                pv[n, :, k : k + DEPTH],
                (((1,), (1,)), ((), ())),
                preferred_element_type=jnp.float32,
            )
        sc = acc * (1.0 / math.sqrt(voxels))
        cols = pl.ds(n * half, half)
        old = top_s[:, cols]
        new = jnp.maximum(old, jnp.max(sc, axis=0, keepdims=True))
        top_s[:, cols] = new
        tot_s[:, cols] = tot_s[:, cols] * jnp.exp(old - new) + jnp.sum(
            jnp.exp(sc - new), axis=0, keepdims=True
        )
        wanted = cid[:, cols] * orients + oid[:, cols]
        inner = lax.broadcasted_iota(jnp.int32, (64, half), 0)
        picked = jnp.zeros((1, half), jnp.float32)
        for i, p in enumerate(group):
            mine = inner == wanted - p * 64
            picked += jnp.sum(
                jnp.where(mine, sc[64 * i : 64 * i + 64], 0.0), axis=0, keepdims=True
            )
        cho_s[:, cols] += picked

    groups = [
        [jnp.where(place == 0, pair(*a), pair(*b)) for a, b in zip(first, second)]
        for first, second in zip(*GROUPS)
    ]
    for s, units in enumerate(UNITS):
        for zc in range(2):

            def branch(s=s, zc=zc):
                run(PLAN[zc][s], zc)
                if s == 0:
                    for h in range(2):
                        send(refs.at[0, pl.ds(16 * h, 16)], own, h, 4)

            pl.when(place == zc)(branch)
        if s == 0:
            for load in loads:
                load.wait()
        for g, n in units:
            if n == 0:
                for p in groups[g]:
                    for h in range(2):
                        block = rows.at[p, 1 - core, h]
                        pltpu.make_async_copy(block, block, sib_sem.at[p, h]).wait()
            scores(n, groups[g])

    gain = wts[...] * (n_cls * orients) * jnp.exp(cho_s[...] - top_s[...]) / tot_s[...]
    gain = gain.astype(jnp.bfloat16).astype(jnp.float32)
    code = (off[...] + SHIFT) * ROWS + cid[...]
    steps = 2 * SHIFT + 1
    which = lax.broadcasted_iota(jnp.int32, (steps * ROWS, 2 * half), 0)
    coef = jnp.where(which == code, gain, 0.0).astype(jnp.bfloat16)
    width = voxels // n_ptl
    lane = lax.broadcasted_iota(jnp.int32, (ROWS, 128), 1) % NX
    for j in range(n_ptl):
        pixels = pv[:, :, j * width : (j + 1) * width].reshape(2 * half, width)
        moved = jnp.dot(coef, pixels, preferred_element_type=jnp.float32)
        for v in range(width // 128):
            total = jnp.zeros((ROWS, 128), jnp.float32)
            for i, step in enumerate(range(-SHIFT, SHIFT + 1)):
                a = moved[i * ROWS : (i + 1) * ROWS, v * 128 : (v + 1) * 128]
                if step == 0:
                    total += a
                    continue
                inside = pltpu.roll(a, step % 128, 1)
                across = pltpu.roll(a, (step + NX) % 128, 1)
                keep = lane >= step if step > 0 else lane < NX + step
                total += jnp.where(keep, inside, across)
            for c in range(n_cls):
                part[c, j : j + 1, v * 128 : (v + 1) * 128] = total[c : c + 1]

    copies = []
    for q in (1, 2, 3):
        copies.append(
            pltpu.make_async_remote_copy(
                src_ref=part.at[column[q]],
                dst_ref=recv1.at[q - 1],
                send_sem=s1_sem.at[q - 1],
                recv_sem=r1_sem.at[q - 1],
                device_id=(column[q], ptl),
                device_id_type=MESH,
            )
        )
        copies[-1].start()
    for copy in copies:
        copy.wait_recv()
    mine = part[cls] + recv1[0] + recv1[1] + recv1[2]
    for j in range(n_ptl):
        send2[j] = mine[j : j + 1]
    for o in range(1, n_ptl):
        to = lax.rem(ptl + o, n_ptl)
        copies.append(
            pltpu.make_async_remote_copy(
                src_ref=send2.at[to],
                dst_ref=recv2.at[o - 1],
                send_sem=s2_sem.at[o - 1],
                recv_sem=r2_sem.at[o - 1],
                device_id=(cls, to),
                device_id_type=MESH,
            )
        )
        copies[-1].start()
    total = send2[ptl]
    for o in range(1, n_ptl):
        copies[2 + o].wait_recv()
        total += recv2[o - 1]
    out[...] = total / jnp.sqrt(jnp.float32(population))
    for copy in copies:
        copy.wait_send()

    def sent(count, idx):
        gone = rows.at[pl.ds(0, count), 0]
        pltpu.make_async_copy(gone, gone, send_sem.at[idx]).wait()

    sent(5, 0)
    sent(5, 1)
    sent(16, 4)

    @pl.when(place == 0)
    def _():
        sent(2, 2)

    @pl.when(place == 1)
    def _():
        sent(3, 2)
        sent(5, 3)


def fused(references, particles, class_ids, orient_ids, offsets, weights):
    n_cls = lax.axis_size("cls")
    n_ptl = lax.axis_size("ptl")
    _, local_ori, voxels = references.shape
    count = particles.shape[0]
    orients = local_ori * n_ptl
    population = count * n_ptl
    line = [x.reshape(1, count) for x in (class_ids, orient_ids, offsets, weights)]
    f32 = jnp.float32
    vmem = pl.BlockSpec(memory_space=pltpu.VMEM)
    hbm = pl.BlockSpec(memory_space=pl.ANY)
    return pl.pallas_call(
        functools.partial(kernel, orients, population),
        out_shape=jax.ShapeDtypeStruct((1, voxels // n_ptl), f32),
        in_specs=[hbm] * 6,
        out_specs=vmem,
        scratch_shapes=[
            pltpu.VMEM((n_cls * n_ptl // 2, 2, 2, local_ori // 2, voxels), references.dtype),
            pltpu.VMEM((2, count // 2, voxels), particles.dtype),
            *[pltpu.VMEM((1, count), x.dtype) for x in line],
            pltpu.VMEM((1, count), f32),
            pltpu.VMEM((1, count), f32),
            pltpu.VMEM((1, count), f32),
            pltpu.VMEM((n_cls, n_ptl, voxels // n_ptl), f32),
            pltpu.VMEM((n_cls - 1, n_ptl, voxels // n_ptl), f32),
            pltpu.VMEM((n_ptl, 1, voxels // n_ptl), f32),
            pltpu.VMEM((n_ptl - 1, 1, voxels // n_ptl), f32),
            pltpu.SemaphoreType.DMA((8,)),
            pltpu.SemaphoreType.DMA((n_cls * n_ptl // 2, 2)),
            pltpu.SemaphoreType.DMA((n_cls * n_ptl // 2, 2)),
            pltpu.SemaphoreType.DMA((5,)),
            pltpu.SemaphoreType.DMA((n_cls - 1,)),
            pltpu.SemaphoreType.DMA((n_ptl - 1,)),
            pltpu.SemaphoreType.DMA((n_cls - 1,)),
            pltpu.SemaphoreType.DMA((n_ptl - 1,)),
        ],
        compiler_params=pltpu.CompilerParams(
            collective_id=0, has_side_effects=True, vmem_limit_bytes=60 * 1024 * 1024
        ),
        cost_estimate=pl.CostEstimate(
            flops=2 * count * voxels * n_cls * orients,
            bytes_accessed=2 * voxels * (count + n_cls * orients),
            transcendentals=count * n_cls * orients,
        ),
    )(references, particles, *line)


def body(references, particles, class_ids, orient_ids, offsets, weights):
    n_cls = lax.axis_size("cls")
    n_ptl = lax.axis_size("ptl")
    per_owner, local_ori, voxels = references.shape
    orients = local_ori * n_ptl
    classes = per_owner * n_cls
    count = particles.shape[0]
    scale = 1.0 / math.sqrt(voxels)
    class_block = lax.all_gather(references, "ptl", axis=1, tiled=True)
    piece = lax.all_gather(class_block, "cls", axis=0, tiled=True)
    rows = piece.reshape(piece.shape[0] * orients, voxels)
    place = jnp.arange(rows.shape[0], dtype=jnp.int32)
    top = jnp.full((count,), -1e30, jnp.float32)
    scores = (
        lax.dot_general(
            particles, rows, (((1,), (1,)), ((), ())), preferred_element_type=jnp.float32
        )
        * scale
    )
    newtop = jnp.maximum(top, jnp.max(scores, axis=1))
    total = jnp.sum(jnp.exp(scores - newtop[:, None]), axis=1)
    picked = (class_ids[:, None] == (place // orients)[None, :]) & (
        orient_ids[:, None] == (place % orients)[None, :]
    )
    chosen = jnp.sum(jnp.where(picked, scores, 0.0), axis=1)
    top, total, chosen = (newtop, total, chosen)
    gain = (weights * (classes * orients) * jnp.exp(chosen - top) / total).astype(jnp.bfloat16)
    member = class_ids[None, :] == jnp.arange(classes, dtype=jnp.int32)[:, None]
    partial_sums = jnp.zeros((classes, voxels), jnp.float32)
    for step in range(-SHIFT, SHIFT + 1):
        coef = jnp.where(
            member & (offsets[None, :] == step), gain[None, :], jnp.zeros((), jnp.bfloat16)
        )
        moved = jnp.dot(coef, particles, preferred_element_type=jnp.float32)
        moved = jnp.roll(moved.reshape(classes, voxels // NX, NX), step, axis=2).reshape(
            classes, voxels
        )
        partial_sums = partial_sums + moved
    owned = lax.psum_scatter(partial_sums, "cls", scatter_dimension=0, tiled=True)
    owned = lax.psum_scatter(owned, "ptl", scatter_dimension=1, tiled=True)
    population = count * n_cls * n_ptl / classes
    return owned / jnp.sqrt(jnp.float32(population))


def solution(mesh):
    placed = (
        P("cls", "ptl", None),
        P(("cls", "ptl"), None),
        P(("cls", "ptl")),
        P(("cls", "ptl")),
        P(("cls", "ptl")),
        P(("cls", "ptl")),
    )
    planned = mesh.shape["cls"] == 4 and mesh.shape["ptl"] == 8
    return jax.shard_map(
        fused if planned else body,
        mesh=mesh,
        in_specs=placed,
        out_specs=P("cls", "ptl"),
        check_vma=False,
    )
```

```python
import functools
import math

import jax
import jax.numpy as jnp
from jax import lax
from jax.experimental import pallas as pl
from jax.experimental.pallas import tpu as pltpu
from jax.sharding import PartitionSpec as P

NX = 64
SHIFT = 3
MESH = pl.DeviceIdType.MESH

PLAN = (
    (
        (
            (0, 0, 1, 0), (0, 0, 0, 1), (0, 0, 0, 2), (0, 0, 0, 0), (0, 0, 1, 1), (0, 0, 1, 2),
        ),
        (
            (0, 1, 0, -1), (2, 0, 0, -1), (1, 0, 1, -1), (2, 0, 0, 0), (1, 0, 1, 1),
        ),
        (
            (0, 1, 0, 1), (0, 1, 1, -1), (2, 0, 1, -1), (1, 0, 0, -1), (0, 1, 1, 0),
        ),
        (
            (0, 1, 0, 0), (0, 1, 1, 1), (0, 2, 0, -1), (3, 0, 1, -1), (3, 0, 0, -1), (3, 0, 1, 2),
            (3, 0, 0, 2),
        ),
        (
            (0, 2, 0, 0), (0, 2, 0, 1), (0, 2, 1, -1), (2, 1, 0, -1), (1, 1, 1, -1),
        ),
        (
            (0, 2, 1, 0), (0, 2, 1, 1), (0, 3, 0, -1), (2, 1, 1, -1), (1, 1, 0, -1),
        ),
        (
            (2, 1, 0, 0), (1, 1, 1, 1), (0, 3, 1, -1), (2, 2, 0, -1), (1, 2, 0, -1),
        ),
        (
            (0, 3, 0, 0), (0, 3, 0, 1), (3, 2, 0, -1), (2, 2, 1, -1), (1, 2, 1, -1),
        ),
        (
            (0, 3, 1, 0), (0, 3, 1, 1), (3, 3, 1, -1), (3, 1, 1, -1), (3, 1, 0, -1),
        ),
        (
            (3, 2, 1, -1), (2, 3, 0, -1), (1, 3, 0, -1),
        ),
        (
            (3, 3, 0, -1), (2, 3, 1, -1), (1, 3, 1, -1),
        ),
    ),
    (
        (
            (0, 1, 1, 0), (0, 1, 0, 1), (0, 1, 0, 2), (0, 1, 0, 3), (0, 1, 0, 0), (0, 1, 1, 1),
            (0, 1, 1, 2), (0, 1, 1, 3),
        ),
        (
            (0, 0, 0, -1), (0, 2, 0, -1), (2, 1, 0, -1), (1, 1, 1, -1), (0, 0, 0, 0), (0, 2, 0, 1),
            (0, 0, 0, 2), (0, 2, 0, 3),
        ),
        (
            (0, 0, 0, 1), (0, 0, 1, -1), (0, 2, 1, -1), (2, 1, 1, -1), (1, 1, 0, -1), (0, 2, 1, 0),
            (0, 0, 1, 2), (0, 2, 1, 3),
        ),
        (
            (1, 1, 1, 1), (0, 3, 0, -1), (2, 2, 0, -1), (1, 0, 0, -1), (2, 2, 0, 0), (0, 3, 0, 3),
        ),
        (
            (0, 2, 0, 0), (0, 3, 1, -1), (2, 0, 0, -1), (1, 2, 1, -1), (1, 2, 1, 1), (0, 3, 1, 3),
            (3, 0, 1, -1), (3, 0, 1, 2),
        ),
        (
            (2, 1, 0, 0), (0, 0, 1, 1), (3, 1, 1, -1), (3, 2, 0, -1), (3, 2, 0, 3), (3, 0, 0, -1),
            (3, 0, 0, 2), (3, 3, 1, -1),
        ),
        (
            (0, 0, 1, 0), (0, 2, 1, 1), (3, 3, 1, 3), (3, 2, 1, -1), (1, 2, 0, -1), (3, 3, 0, -1),
        ),
        (
            (0, 3, 0, 0), (0, 3, 0, 1), (3, 2, 1, 3), (2, 0, 1, -1), (3, 1, 0, -1),
        ),
        (
            (0, 3, 1, 0), (0, 3, 1, 1), (3, 3, 0, 3), (2, 2, 1, -1), (1, 0, 1, -1),
        ),
        (
            (2, 3, 0, -1), (1, 3, 0, -1),
        ),
        (
            (2, 3, 1, -1), (1, 3, 1, -1),
        ),
    ),
)

BLOCKS = (
    (
        ((0, 0), (0, 1), (2, 0), (1, 0)),
        ((3, 0), (0, 2), (2, 1), (1, 1)),
        ((0, 3), (2, 2), (1, 2), (3, 1)),
        ((3, 2), (3, 3), (2, 3), (1, 3)),
    ),
    (
        ((0, 1), (0, 0), (0, 2), (2, 1)),
        ((1, 1), (0, 3), (3, 0), (1, 2)),
        ((3, 2), (3, 3), (2, 0), (3, 1)),
        ((2, 2), (1, 0), (2, 3), (1, 3)),
    ),
)
GROUPS = (
    *(tuple((g, i, h) for i in range(4) for h in range(2)) for g in range(3)),
    ((3, 0, 0), (3, 0, 1), (3, 1, 1), (3, 2, 0), (3, 3, 0)),
    ((3, 1, 0), (3, 2, 1), (3, 3, 1)),
)
UNITS = (
    (),
    (),
    ((0, 0),),
    ((0, 1),),
    (),
    (),
    ((1, 0),),
    ((1, 1),),
    ((2, 0), (2, 1)),
    ((3, 0), (3, 1)),
    ((4, 0), (4, 1)),
)
DEPTH = 1024
ROWS = 8


def kernel(
    orients, population,
    refs, parts, cid_in, oid_in, off_in, wts_in, out,
    rows, pv, cid, oid, off, wts, top_s, tot_s, cho_s, part, recv1, send2, recv2,
    local_sem, ici_sem, sib_sem, send_sem, r1_sem, r2_sem, s1_sem, s2_sem,
):
    n_cls, n_ptl = part.shape[0], part.shape[1]
    voxels = refs.shape[2]
    half = pv.shape[1]
    cls, ptl = lax.axis_index("cls"), lax.axis_index("ptl")
    core, z = ptl % 2, ptl // 2
    far = z // 2
    sign = 1 - 2 * far
    place = z + far * (3 - 2 * z)
    along_x = cls + 1 - 2 * (cls % 2)
    along_y = cls + 2 - 4 * (cls // 2)
    column = (cls, along_x, along_y, 3 - cls)
    sibling = (cls, ptl + 1 - 2 * core)
    ways = (
        (along_x, ptl),
        (along_y, ptl),
        (cls, ptl + 2 * sign),
        (cls, ptl - 2 * sign),
    )

    def pair(q, zz):
        return column[q] * 4 + zz + far * (3 - 2 * zz)

    barrier = pltpu.get_barrier_semaphore()
    for q in (1, 2, 3):
        pl.semaphore_signal(barrier, inc=1, device_id=(column[q], ptl), device_id_type=MESH)
    for o in range(1, n_ptl):
        pl.semaphore_signal(
            barrier, inc=1, device_id=(cls, lax.rem(ptl + o, n_ptl)), device_id_type=MESH
        )
    loads = [
        pltpu.make_async_copy(parts.at[pl.ds(i * half, half)], pv.at[i], local_sem.at[i])
        for i in range(2)
    ]
    own = cls * 4 + z
    for h in range(2):
        loads.append(
            pltpu.make_async_copy(
                refs.at[0, pl.ds(16 * h, 16)], rows.at[own, core, h], local_sem.at[2 + h]
            )
        )
    for i, (a, b) in enumerate(((cid_in, cid), (oid_in, oid), (off_in, off), (wts_in, wts))):
        loads.append(pltpu.make_async_copy(a, b, local_sem.at[4 + i]))
    for load in loads:
        load.start()
    pl.semaphore_wait(barrier, 3 + n_ptl - 1)

    def send(src, p, h, way):
        target, recv, idx = (
            (sibling, sib_sem, 4) if way == 4 else (ways[way], ici_sem, way)
        )
        pltpu.make_async_remote_copy(
            src_ref=src,
            dst_ref=rows.at[p, core, h],
            send_sem=send_sem.at[idx],
            recv_sem=recv.at[p, h],
            device_id=target,
            device_id_type=MESH,
        ).start()

    def run(section, zc):
        for q, zz, h, way in section:
            p = pair(q, zz)
            block = rows.at[p, core, h]
            if way < 0:
                pltpu.make_async_copy(block, block, ici_sem.at[p, h]).wait()
                send(block, p, h, 4)
            elif q == 0 and zz == zc:
                send(refs.at[0, pl.ds(16 * h, 16)], p, h, way)
            else:
                send(block, p, h, way)

    top_s[...] = jnp.full(top_s.shape, -jnp.inf, jnp.float32)
    tot_s[...] = jnp.zeros(tot_s.shape, jnp.float32)
    cho_s[...] = jnp.zeros(cho_s.shape, jnp.float32)

    def scores(n, group):
        acc = jnp.zeros((len(group) * 32, half), jnp.float32)
        for k in range(0, voxels, DEPTH):
            lhs = jnp.concatenate(
                [rows[p, :, h, :, k : k + DEPTH].reshape(32, DEPTH) for p, h in group], axis=0
            )
            acc += lax.dot_general(
                lhs,
                pv[n, :, k : k + DEPTH],
                (((1,), (1,)), ((), ())),
                preferred_element_type=jnp.float32,
            )
        sc = acc * (1.0 / math.sqrt(voxels))
        cols = pl.ds(n * half, half)
        old = top_s[:, cols]
        new = jnp.maximum(old, jnp.max(sc, axis=0, keepdims=True))
        top_s[:, cols] = new
        tot_s[:, cols] = tot_s[:, cols] * jnp.exp(old - new) + jnp.sum(
            jnp.exp(sc - new), axis=0, keepdims=True
        )
        wanted = cid[:, cols] * orients + oid[:, cols]
        row = lax.broadcasted_iota(jnp.int32, (32, half), 0)
        inner = row + row // 16 * 16
        picked = jnp.zeros((1, half), jnp.float32)
        for i, (p, h) in enumerate(group):
            mine = inner == wanted - (p * 64 + h * 16)
            picked += jnp.sum(
                jnp.where(mine, sc[32 * i : 32 * i + 32], 0.0), axis=0, keepdims=True
            )
        cho_s[:, cols] += picked

    places = [
        [jnp.where(place == 0, pair(*a), pair(*b)) for a, b in zip(first, second)]
        for first, second in zip(*BLOCKS)
    ]
    groups = [[(places[g][i], h) for g, i, h in group] for group in GROUPS]
    for s, units in enumerate(UNITS):
        for zc in range(2):

            def branch(s=s, zc=zc):
                run(PLAN[zc][s], zc)
                if s == 0:
                    for h in range(2):
                        send(refs.at[0, pl.ds(16 * h, 16)], own, h, 4)

            pl.when(place == zc)(branch)
        if s == 0:
            for load in loads:
                load.wait()
        for g, n in units:
            if n == 0:
                for p, h in groups[g]:
                    block = rows.at[p, 1 - core, h]
                    pltpu.make_async_copy(block, block, sib_sem.at[p, h]).wait()
            scores(n, groups[g])

    gain = wts[...] * (n_cls * orients) * jnp.exp(cho_s[...] - top_s[...]) / tot_s[...]
    gain = gain.astype(jnp.bfloat16).astype(jnp.float32)
    code = (off[...] + SHIFT) * ROWS + cid[...]
    steps = 2 * SHIFT + 1
    which = lax.broadcasted_iota(jnp.int32, (steps * ROWS, 2 * half), 0)
    coef = jnp.where(which == code, gain, 0.0).astype(jnp.bfloat16)
    width = voxels // n_ptl
    lane = lax.broadcasted_iota(jnp.int32, (ROWS, 128), 1) % NX
    for j in range(n_ptl):
        pixels = pv[:, :, j * width : (j + 1) * width].reshape(2 * half, width)
        moved = jnp.dot(coef, pixels, preferred_element_type=jnp.float32)
        for v in range(width // 128):
            total = jnp.zeros((ROWS, 128), jnp.float32)
            for i, step in enumerate(range(-SHIFT, SHIFT + 1)):
                a = moved[i * ROWS : (i + 1) * ROWS, v * 128 : (v + 1) * 128]
                if step == 0:
                    total += a
                    continue
                inside = pltpu.roll(a, step % 128, 1)
                across = pltpu.roll(a, (step + NX) % 128, 1)
                keep = lane >= step if step > 0 else lane < NX + step
                total += jnp.where(keep, inside, across)
            for c in range(n_cls):
                part[c, j : j + 1, v * 128 : (v + 1) * 128] = total[c : c + 1]

    copies = []
    for q in (1, 2, 3):
        copies.append(
            pltpu.make_async_remote_copy(
                src_ref=part.at[column[q]],
                dst_ref=recv1.at[q - 1],
                send_sem=s1_sem.at[q - 1],
                recv_sem=r1_sem.at[q - 1],
                device_id=(column[q], ptl),
                device_id_type=MESH,
            )
        )
        copies[-1].start()
    for copy in copies:
        copy.wait_recv()
    mine = part[cls] + recv1[0] + recv1[1] + recv1[2]
    for j in range(n_ptl):
        send2[j] = mine[j : j + 1]
    for o in range(1, n_ptl):
        to = lax.rem(ptl + o, n_ptl)
        copies.append(
            pltpu.make_async_remote_copy(
                src_ref=send2.at[to],
                dst_ref=recv2.at[o - 1],
                send_sem=s2_sem.at[o - 1],
                recv_sem=r2_sem.at[o - 1],
                device_id=(cls, to),
                device_id_type=MESH,
            )
        )
        copies[-1].start()
    total = send2[ptl]
    for o in range(1, n_ptl):
        copies[2 + o].wait_recv()
        total += recv2[o - 1]
    out[...] = total / jnp.sqrt(jnp.float32(population))
    for copy in copies:
        copy.wait_send()

    def sent(count, idx):
        gone = rows.at[pl.ds(0, count), 0]
        pltpu.make_async_copy(gone, gone, send_sem.at[idx]).wait()

    sent(5, 0)
    sent(5, 1)
    sent(16, 4)

    @pl.when(place == 0)
    def _():
        sent(2, 2)

    @pl.when(place == 1)
    def _():
        sent(3, 2)
        sent(5, 3)


def fused(references, particles, class_ids, orient_ids, offsets, weights):
    n_cls = lax.axis_size("cls")
    n_ptl = lax.axis_size("ptl")
    _, local_ori, voxels = references.shape
    count = particles.shape[0]
    orients = local_ori * n_ptl
    population = count * n_ptl
    line = [x.reshape(1, count) for x in (class_ids, orient_ids, offsets, weights)]
    f32 = jnp.float32
    vmem = pl.BlockSpec(memory_space=pltpu.VMEM)
    hbm = pl.BlockSpec(memory_space=pl.ANY)
    return pl.pallas_call(
        functools.partial(kernel, orients, population),
        out_shape=jax.ShapeDtypeStruct((1, voxels // n_ptl), f32),
        in_specs=[hbm] * 6,
        out_specs=vmem,
        scratch_shapes=[
            pltpu.VMEM((n_cls * n_ptl // 2, 2, 2, local_ori // 2, voxels), references.dtype),
            pltpu.VMEM((2, count // 2, voxels), particles.dtype),
            *[pltpu.VMEM((1, count), x.dtype) for x in line],
            pltpu.VMEM((1, count), f32),
            pltpu.VMEM((1, count), f32),
            pltpu.VMEM((1, count), f32),
            pltpu.VMEM((n_cls, n_ptl, voxels // n_ptl), f32),
            pltpu.VMEM((n_cls - 1, n_ptl, voxels // n_ptl), f32),
            pltpu.VMEM((n_ptl, 1, voxels // n_ptl), f32),
            pltpu.VMEM((n_ptl - 1, 1, voxels // n_ptl), f32),
            pltpu.SemaphoreType.DMA((8,)),
            pltpu.SemaphoreType.DMA((n_cls * n_ptl // 2, 2)),
            pltpu.SemaphoreType.DMA((n_cls * n_ptl // 2, 2)),
            pltpu.SemaphoreType.DMA((5,)),
            pltpu.SemaphoreType.DMA((n_cls - 1,)),
            pltpu.SemaphoreType.DMA((n_ptl - 1,)),
            pltpu.SemaphoreType.DMA((n_cls - 1,)),
            pltpu.SemaphoreType.DMA((n_ptl - 1,)),
        ],
        compiler_params=pltpu.CompilerParams(
            collective_id=0, has_side_effects=True, vmem_limit_bytes=60 * 1024 * 1024
        ),
        cost_estimate=pl.CostEstimate(
            flops=2 * count * voxels * n_cls * orients,
            bytes_accessed=2 * voxels * (count + n_cls * orients),
            transcendentals=count * n_cls * orients,
        ),
    )(references, particles, *line)


def body(references, particles, class_ids, orient_ids, offsets, weights):
    n_cls = lax.axis_size("cls")
    n_ptl = lax.axis_size("ptl")
    per_owner, local_ori, voxels = references.shape
    orients = local_ori * n_ptl
    classes = per_owner * n_cls
    count = particles.shape[0]
    scale = 1.0 / math.sqrt(voxels)
    class_block = lax.all_gather(references, "ptl", axis=1, tiled=True)
    piece = lax.all_gather(class_block, "cls", axis=0, tiled=True)
    rows = piece.reshape(piece.shape[0] * orients, voxels)
    place = jnp.arange(rows.shape[0], dtype=jnp.int32)
    top = jnp.full((count,), -1e30, jnp.float32)
    scores = (
        lax.dot_general(
            particles, rows, (((1,), (1,)), ((), ())), preferred_element_type=jnp.float32
        )
        * scale
    )
    newtop = jnp.maximum(top, jnp.max(scores, axis=1))
    total = jnp.sum(jnp.exp(scores - newtop[:, None]), axis=1)
    picked = (class_ids[:, None] == (place // orients)[None, :]) & (
        orient_ids[:, None] == (place % orients)[None, :]
    )
    chosen = jnp.sum(jnp.where(picked, scores, 0.0), axis=1)
    top, total, chosen = (newtop, total, chosen)
    gain = (weights * (classes * orients) * jnp.exp(chosen - top) / total).astype(jnp.bfloat16)
    member = class_ids[None, :] == jnp.arange(classes, dtype=jnp.int32)[:, None]
    partial_sums = jnp.zeros((classes, voxels), jnp.float32)
    for step in range(-SHIFT, SHIFT + 1):
        coef = jnp.where(
            member & (offsets[None, :] == step), gain[None, :], jnp.zeros((), jnp.bfloat16)
        )
        moved = jnp.dot(coef, particles, preferred_element_type=jnp.float32)
        moved = jnp.roll(moved.reshape(classes, voxels // NX, NX), step, axis=2).reshape(
            classes, voxels
        )
        partial_sums = partial_sums + moved
    owned = lax.psum_scatter(partial_sums, "cls", scatter_dimension=0, tiled=True)
    owned = lax.psum_scatter(owned, "ptl", scatter_dimension=1, tiled=True)
    population = count * n_cls * n_ptl / classes
    return owned / jnp.sqrt(jnp.float32(population))


def solution(mesh):
    placed = (
        P("cls", "ptl", None),
        P(("cls", "ptl"), None),
        P(("cls", "ptl")),
        P(("cls", "ptl")),
        P(("cls", "ptl")),
        P(("cls", "ptl")),
    )
    planned = mesh.shape["cls"] == 4 and mesh.shape["ptl"] == 8
    return jax.shard_map(
        fused if planned else body,
        mesh=mesh,
        in_specs=placed,
        out_specs=P("cls", "ptl"),
        check_vma=False,
    )
```

```python
import functools
import math

import jax
import jax.numpy as jnp
from jax import lax
from jax.experimental import pallas as pl
from jax.experimental.pallas import tpu as pltpu
from jax.sharding import PartitionSpec as P

NX = 64
SHIFT = 3
MESH = pl.DeviceIdType.MESH

PLAN = (
    (
        (
            (0, 0, 1, 0), (0, 0, 0, 1), (0, 0, 0, 2), (0, 0, 0, 0), (0, 0, 1, 1), (0, 0, 1, 2),
        ),
        (
            (0, 1, 0, -1), (2, 0, 0, -1), (1, 0, 1, -1), (2, 0, 0, 0), (1, 0, 1, 1),
        ),
        (
            (0, 1, 0, 1), (0, 1, 1, -1), (2, 0, 1, -1), (1, 0, 0, -1), (0, 1, 1, 0),
        ),
        (
            (0, 1, 0, 0), (0, 1, 1, 1), (0, 2, 0, -1), (3, 0, 1, -1), (3, 0, 0, -1), (3, 0, 1, 2),
            (3, 0, 0, 2),
        ),
        (
            (0, 2, 0, 0), (0, 2, 0, 1), (0, 2, 1, -1), (2, 1, 0, -1), (1, 1, 1, -1),
        ),
        (
            (0, 2, 1, 0), (0, 2, 1, 1), (0, 3, 0, -1), (2, 1, 1, -1), (1, 1, 0, -1),
        ),
        (
            (2, 1, 0, 0), (1, 1, 1, 1), (0, 3, 1, -1), (2, 2, 0, -1), (1, 2, 0, -1),
        ),
        (
            (0, 3, 0, 0), (0, 3, 0, 1), (3, 2, 0, -1), (2, 2, 1, -1), (1, 2, 1, -1),
        ),
        (
            (0, 3, 1, 0), (0, 3, 1, 1), (3, 3, 1, -1), (3, 1, 1, -1), (3, 1, 0, -1),
        ),
        (
            (3, 2, 1, -1), (2, 3, 0, -1), (1, 3, 0, -1),
        ),
        (
            (3, 3, 0, -1), (2, 3, 1, -1), (1, 3, 1, -1),
        ),
    ),
    (
        (
            (0, 1, 1, 0), (0, 1, 0, 1), (0, 1, 0, 2), (0, 1, 0, 3), (0, 1, 0, 0), (0, 1, 1, 1),
            (0, 1, 1, 2), (0, 1, 1, 3),
        ),
        (
            (0, 0, 0, -1), (0, 2, 0, -1), (2, 1, 0, -1), (1, 1, 1, -1), (0, 0, 0, 0), (0, 2, 0, 1),
            (0, 0, 0, 2), (0, 2, 0, 3),
        ),
        (
            (0, 0, 0, 1), (0, 0, 1, -1), (0, 2, 1, -1), (2, 1, 1, -1), (1, 1, 0, -1), (0, 2, 1, 0),
            (0, 0, 1, 2), (0, 2, 1, 3),
        ),
        (
            (1, 1, 1, 1), (0, 3, 0, -1), (2, 2, 0, -1), (1, 0, 0, -1), (2, 2, 0, 0), (0, 3, 0, 3),
        ),
        (
            (0, 2, 0, 0), (0, 3, 1, -1), (2, 0, 0, -1), (1, 2, 1, -1), (1, 2, 1, 1), (0, 3, 1, 3),
            (3, 0, 1, -1), (3, 0, 1, 2),
        ),
        (
            (2, 1, 0, 0), (0, 0, 1, 1), (3, 1, 1, -1), (3, 2, 0, -1), (3, 2, 0, 3), (3, 0, 0, -1),
            (3, 0, 0, 2), (3, 3, 1, -1),
        ),
        (
            (0, 0, 1, 0), (0, 2, 1, 1), (3, 3, 1, 3), (3, 2, 1, -1), (1, 2, 0, -1), (3, 3, 0, -1),
        ),
        (
            (0, 3, 0, 0), (0, 3, 0, 1), (3, 2, 1, 3), (2, 0, 1, -1), (3, 1, 0, -1),
        ),
        (
            (0, 3, 1, 0), (0, 3, 1, 1), (3, 3, 0, 3), (2, 2, 1, -1), (1, 0, 1, -1),
        ),
        (
            (2, 3, 0, -1), (1, 3, 0, -1),
        ),
        (
            (2, 3, 1, -1), (1, 3, 1, -1),
        ),
    ),
)

GROUPS = (
    (
        ((0, 0), (0, 1), (2, 0), (1, 0)),
        ((3, 0), (0, 2), (2, 1), (1, 1)),
        ((0, 3), (2, 2), (1, 2), (3, 1)),
        ((3, 2), (2, 3), (1, 3), (3, 3)),
    ),
    (
        ((0, 1), (0, 0), (0, 2), (2, 1)),
        ((1, 1), (0, 3), (3, 0), (1, 2)),
        ((3, 2), (3, 3), (2, 0), (3, 1)),
        ((2, 2), (1, 0), (2, 3), (1, 3)),
    ),
)
UNITS = ((), (), (0,), (), (), (), (1,), (), (2,), (), (3,))
DEPTH = 1024
ROWS = 8


def kernel(
    orients, population,
    refs, parts, cid_in, oid_in, off_in, wts_in, out,
    rows, pv, cid, oid, off, wts, top_s, tot_s, cho_s, part, recv1, send2, recv2,
    local_sem, ici_sem, sib_sem, send_sem, r1_sem, r2_sem, s1_sem, s2_sem,
):
    n_cls, n_ptl = part.shape[0], part.shape[1]
    voxels = refs.shape[2]
    half = pv.shape[1]
    cls, ptl = lax.axis_index("cls"), lax.axis_index("ptl")
    core, z = ptl % 2, ptl // 2
    far = z // 2
    sign = 1 - 2 * far
    place = z + far * (3 - 2 * z)
    along_x = cls + 1 - 2 * (cls % 2)
    along_y = cls + 2 - 4 * (cls // 2)
    column = (cls, along_x, along_y, 3 - cls)
    sibling = (cls, ptl + 1 - 2 * core)
    ways = (
        (along_x, ptl),
        (along_y, ptl),
        (cls, ptl + 2 * sign),
        (cls, ptl - 2 * sign),
    )

    def pair(q, zz):
        return column[q] * 4 + zz + far * (3 - 2 * zz)

    barrier = pltpu.get_barrier_semaphore()
    for q in (1, 2, 3):
        pl.semaphore_signal(barrier, inc=1, device_id=(column[q], ptl), device_id_type=MESH)
    for o in range(1, n_ptl):
        pl.semaphore_signal(
            barrier, inc=1, device_id=(cls, lax.rem(ptl + o, n_ptl)), device_id_type=MESH
        )
    loads = [
        pltpu.make_async_copy(parts.at[pl.ds(i * half, half)], pv.at[i], local_sem.at[i])
        for i in range(2)
    ]
    own = cls * 4 + z
    for h in range(2):
        loads.append(
            pltpu.make_async_copy(
                refs.at[0, pl.ds(16 * h, 16)], rows.at[own, core, h], local_sem.at[2 + h]
            )
        )
    for i, (a, b) in enumerate(((cid_in, cid), (oid_in, oid), (off_in, off), (wts_in, wts))):
        loads.append(pltpu.make_async_copy(a, b, local_sem.at[4 + i]))
    for load in loads:
        load.start()
    pl.semaphore_wait(barrier, 3 + n_ptl - 1)

    def send(src, p, h, way):
        target, recv, idx = (
            (sibling, sib_sem, 4) if way == 4 else (ways[way], ici_sem, way)
        )
        pltpu.make_async_remote_copy(
            src_ref=src,
            dst_ref=rows.at[p, core, h],
            send_sem=send_sem.at[idx],
            recv_sem=recv.at[p, h],
            device_id=target,
            device_id_type=MESH,
        ).start()

    def run(section, zc):
        for q, zz, h, way in section:
            p = pair(q, zz)
            block = rows.at[p, core, h]
            if way < 0:
                pltpu.make_async_copy(block, block, ici_sem.at[p, h]).wait()
                send(block, p, h, 4)
            elif q == 0 and zz == zc:
                send(refs.at[0, pl.ds(16 * h, 16)], p, h, way)
            else:
                send(block, p, h, way)

    top_s[...] = jnp.full(top_s.shape, -jnp.inf, jnp.float32)
    tot_s[...] = jnp.zeros(tot_s.shape, jnp.float32)
    cho_s[...] = jnp.zeros(cho_s.shape, jnp.float32)

    def scores(group):
        acc = jnp.zeros((2 * half, len(group) * 64), jnp.float32)
        for k in range(0, voxels, DEPTH):
            block = jnp.concatenate(
                [rows[p, :, :, :, k : k + DEPTH].reshape(64, DEPTH) for p in group], axis=0
            )
            acc += lax.dot_general(
                pv[:, :, k : k + DEPTH].reshape(2 * half, DEPTH),
                block,
                (((1,), (1,)), ((), ())),
                preferred_element_type=jnp.float32,
            )
        sc = acc.T * (1.0 / math.sqrt(voxels))
        old = top_s[...]
        new = jnp.maximum(old, jnp.max(sc, axis=0, keepdims=True))
        top_s[...] = new
        tot_s[...] = tot_s[...] * jnp.exp(old - new) + jnp.sum(
            jnp.exp(sc - new), axis=0, keepdims=True
        )
        wanted = cid[...] * orients + oid[...]
        inner = lax.broadcasted_iota(jnp.int32, (64, 2 * half), 0)
        picked = jnp.zeros((1, 2 * half), jnp.float32)
        for i, p in enumerate(group):
            mine = inner == wanted - p * 64
            picked += jnp.sum(
                jnp.where(mine, sc[64 * i : 64 * i + 64], 0.0), axis=0, keepdims=True
            )
        cho_s[...] += picked

    groups = [
        [jnp.where(place == 0, pair(*a), pair(*b)) for a, b in zip(first, second)]
        for first, second in zip(*GROUPS)
    ]
    for s, units in enumerate(UNITS):
        for zc in range(2):

            def branch(s=s, zc=zc):
                run(PLAN[zc][s], zc)
                if s == 0:
                    for h in range(2):
                        send(refs.at[0, pl.ds(16 * h, 16)], own, h, 4)

            pl.when(place == zc)(branch)
        if s == 0:
            for load in loads:
                load.wait()
        for g in units:
            for p in groups[g]:
                for h in range(2):
                    block = rows.at[p, 1 - core, h]
                    pltpu.make_async_copy(block, block, sib_sem.at[p, h]).wait()
            scores(groups[g])

    gain = wts[...] * (n_cls * orients) * jnp.exp(cho_s[...] - top_s[...]) / tot_s[...]
    gain = gain.astype(jnp.bfloat16).astype(jnp.float32)
    code = (off[...] + SHIFT) * ROWS + cid[...]
    steps = 2 * SHIFT + 1
    which = lax.broadcasted_iota(jnp.int32, (steps * ROWS, 2 * half), 0)
    coef = jnp.where(which == code, gain, 0.0).astype(jnp.bfloat16)
    width = voxels // n_ptl
    lane = lax.broadcasted_iota(jnp.int32, (ROWS, 128), 1) % NX
    for j in range(n_ptl):
        pixels = pv[:, :, j * width : (j + 1) * width].reshape(2 * half, width)
        moved = jnp.dot(coef, pixels, preferred_element_type=jnp.float32)
        for v in range(width // 128):
            total = jnp.zeros((ROWS, 128), jnp.float32)
            for i, step in enumerate(range(-SHIFT, SHIFT + 1)):
                a = moved[i * ROWS : (i + 1) * ROWS, v * 128 : (v + 1) * 128]
                if step == 0:
                    total += a
                    continue
                inside = pltpu.roll(a, step % 128, 1)
                across = pltpu.roll(a, (step + NX) % 128, 1)
                keep = lane >= step if step > 0 else lane < NX + step
                total += jnp.where(keep, inside, across)
            for c in range(n_cls):
                part[c, j : j + 1, v * 128 : (v + 1) * 128] = total[c : c + 1]

    copies = []
    for q in (1, 2, 3):
        copies.append(
            pltpu.make_async_remote_copy(
                src_ref=part.at[column[q]],
                dst_ref=recv1.at[q - 1],
                send_sem=s1_sem.at[q - 1],
                recv_sem=r1_sem.at[q - 1],
                device_id=(column[q], ptl),
                device_id_type=MESH,
            )
        )
        copies[-1].start()
    for copy in copies:
        copy.wait_recv()
    mine = part[cls] + recv1[0] + recv1[1] + recv1[2]
    for j in range(n_ptl):
        send2[j] = mine[j : j + 1]
    for o in range(1, n_ptl):
        to = lax.rem(ptl + o, n_ptl)
        copies.append(
            pltpu.make_async_remote_copy(
                src_ref=send2.at[to],
                dst_ref=recv2.at[o - 1],
                send_sem=s2_sem.at[o - 1],
                recv_sem=r2_sem.at[o - 1],
                device_id=(cls, to),
                device_id_type=MESH,
            )
        )
        copies[-1].start()
    total = send2[ptl]
    for o in range(1, n_ptl):
        copies[2 + o].wait_recv()
        total += recv2[o - 1]
    out[...] = total / jnp.sqrt(jnp.float32(population))
    for copy in copies:
        copy.wait_send()

    def sent(count, idx):
        gone = rows.at[pl.ds(0, count), 0]
        pltpu.make_async_copy(gone, gone, send_sem.at[idx]).wait()

    sent(5, 0)
    sent(5, 1)
    sent(16, 4)

    @pl.when(place == 0)
    def _():
        sent(2, 2)

    @pl.when(place == 1)
    def _():
        sent(3, 2)
        sent(5, 3)


def fused(references, particles, class_ids, orient_ids, offsets, weights):
    n_cls = lax.axis_size("cls")
    n_ptl = lax.axis_size("ptl")
    _, local_ori, voxels = references.shape
    count = particles.shape[0]
    orients = local_ori * n_ptl
    population = count * n_ptl
    line = [x.reshape(1, count) for x in (class_ids, orient_ids, offsets, weights)]
    f32 = jnp.float32
    vmem = pl.BlockSpec(memory_space=pltpu.VMEM)
    hbm = pl.BlockSpec(memory_space=pl.ANY)
    return pl.pallas_call(
        functools.partial(kernel, orients, population),
        out_shape=jax.ShapeDtypeStruct((1, voxels // n_ptl), f32),
        in_specs=[hbm] * 6,
        out_specs=vmem,
        scratch_shapes=[
            pltpu.VMEM((n_cls * n_ptl // 2, 2, 2, local_ori // 2, voxels), references.dtype),
            pltpu.VMEM((2, count // 2, voxels), particles.dtype),
            *[pltpu.VMEM((1, count), x.dtype) for x in line],
            pltpu.VMEM((1, count), f32),
            pltpu.VMEM((1, count), f32),
            pltpu.VMEM((1, count), f32),
            pltpu.VMEM((n_cls, n_ptl, voxels // n_ptl), f32),
            pltpu.VMEM((n_cls - 1, n_ptl, voxels // n_ptl), f32),
            pltpu.VMEM((n_ptl, 1, voxels // n_ptl), f32),
            pltpu.VMEM((n_ptl - 1, 1, voxels // n_ptl), f32),
            pltpu.SemaphoreType.DMA((8,)),
            pltpu.SemaphoreType.DMA((n_cls * n_ptl // 2, 2)),
            pltpu.SemaphoreType.DMA((n_cls * n_ptl // 2, 2)),
            pltpu.SemaphoreType.DMA((5,)),
            pltpu.SemaphoreType.DMA((n_cls - 1,)),
            pltpu.SemaphoreType.DMA((n_ptl - 1,)),
            pltpu.SemaphoreType.DMA((n_cls - 1,)),
            pltpu.SemaphoreType.DMA((n_ptl - 1,)),
        ],
        compiler_params=pltpu.CompilerParams(
            collective_id=0, has_side_effects=True, vmem_limit_bytes=60 * 1024 * 1024
        ),
        cost_estimate=pl.CostEstimate(
            flops=2 * count * voxels * n_cls * orients,
            bytes_accessed=2 * voxels * (count + n_cls * orients),
            transcendentals=count * n_cls * orients,
        ),
    )(references, particles, *line)


def body(references, particles, class_ids, orient_ids, offsets, weights):
    n_cls = lax.axis_size("cls")
    n_ptl = lax.axis_size("ptl")
    per_owner, local_ori, voxels = references.shape
    orients = local_ori * n_ptl
    classes = per_owner * n_cls
    count = particles.shape[0]
    scale = 1.0 / math.sqrt(voxels)
    class_block = lax.all_gather(references, "ptl", axis=1, tiled=True)
    piece = lax.all_gather(class_block, "cls", axis=0, tiled=True)
    rows = piece.reshape(piece.shape[0] * orients, voxels)
    place = jnp.arange(rows.shape[0], dtype=jnp.int32)
    top = jnp.full((count,), -1e30, jnp.float32)
    scores = (
        lax.dot_general(
            particles, rows, (((1,), (1,)), ((), ())), preferred_element_type=jnp.float32
        )
        * scale
    )
    newtop = jnp.maximum(top, jnp.max(scores, axis=1))
    total = jnp.sum(jnp.exp(scores - newtop[:, None]), axis=1)
    picked = (class_ids[:, None] == (place // orients)[None, :]) & (
        orient_ids[:, None] == (place % orients)[None, :]
    )
    chosen = jnp.sum(jnp.where(picked, scores, 0.0), axis=1)
    top, total, chosen = (newtop, total, chosen)
    gain = (weights * (classes * orients) * jnp.exp(chosen - top) / total).astype(jnp.bfloat16)
    member = class_ids[None, :] == jnp.arange(classes, dtype=jnp.int32)[:, None]
    partial_sums = jnp.zeros((classes, voxels), jnp.float32)
    for step in range(-SHIFT, SHIFT + 1):
        coef = jnp.where(
            member & (offsets[None, :] == step), gain[None, :], jnp.zeros((), jnp.bfloat16)
        )
        moved = jnp.dot(coef, particles, preferred_element_type=jnp.float32)
        moved = jnp.roll(moved.reshape(classes, voxels // NX, NX), step, axis=2).reshape(
            classes, voxels
        )
        partial_sums = partial_sums + moved
    owned = lax.psum_scatter(partial_sums, "cls", scatter_dimension=0, tiled=True)
    owned = lax.psum_scatter(owned, "ptl", scatter_dimension=1, tiled=True)
    population = count * n_cls * n_ptl / classes
    return owned / jnp.sqrt(jnp.float32(population))


def solution(mesh):
    placed = (
        P("cls", "ptl", None),
        P(("cls", "ptl"), None),
        P(("cls", "ptl")),
        P(("cls", "ptl")),
        P(("cls", "ptl")),
        P(("cls", "ptl")),
    )
    planned = mesh.shape["cls"] == 4 and mesh.shape["ptl"] == 8
    return jax.shard_map(
        fused if planned else body,
        mesh=mesh,
        in_specs=placed,
        out_specs=P("cls", "ptl"),
        check_vma=False,
    )
```
